256 devices in a mesh: row: 8 (over y, x_hi), col: 32 (over z, x_lo, core).
Axes of the slice: x: 4 (x_hi: 2, x_lo: 2; x = x_hi * 2 + x_lo), y: 4, z: 8, core: 2. Of those that a mesh axis runs over, the one named last changes fastest.
Arguments:
- vectors: bfloat16 [8, 131072], P(None, ('col', 'row')), may hold values from -6 to 6
- energies: float32 [131072], P(('col', 'row')), may hold values from 0.5 to 3
- tiles: bfloat16 [8, 32, 256, 128, 128], P('row', 'col'), may hold values from -0.09375 to 0.09375
- tile_rows: int32 [8, 32, 256], P('row', 'col'), may hold values from 0 to 127, as said below
- tile_cols: int32 [8, 32, 256], P('row', 'col'), may hold values from 0 to 31
- counts: int32 [8, 32], P('row', 'col'), may hold values from 1 to 256, as said below
Outputs:
- product: bfloat16 [8, 131072], P(None, ('col', 'row'))
The draws below stay inside these ranges and needn't reach their ends.
Inputs may be any that keep to these rules, and one draw needn't show every extreme that they name: `tile_rows`: a // 4 <= c on device (r, c), and I <= J for every slot: only the upper block triangle is stored. `counts`: slots at or past a device's count are ignored; some device has all 256 slots live.
All inputs are finite; a program needn't handle non-finite values.
Results may differ from the reference program's by a relative error of at most 0.0013.
Values may be sent and summed in bfloat16 or wider, within the bound.
A program may use at most 64 MiB of HBM per device.

```python
import jax
import jax.numpy as jnp
from jax import lax

NVEC = 8
TILE = 128
SUB = 4
TILES_DEV = 256
GRID_ROWS = 8
GRID_COLS = 32
M = 131072


def place_tiles(key):
    key_seg, key_sub, key_col = jax.random.split(key, 3)
    shape = (GRID_ROWS, GRID_COLS, TILES_DEV)
    col_dev = jnp.arange(GRID_COLS).astype(jnp.int32)[None, :, None] * jnp.ones(shape, jnp.int32)
    row_dev = jnp.arange(GRID_ROWS).astype(jnp.int32)[:, None, None] * jnp.ones(shape, jnp.int32)
    segment = jax.random.randint(key_seg, shape, 0, col_dev + 1)
    within = jax.random.randint(key_sub, shape, 0, SUB)
    lowest = jnp.where(segment == col_dev, row_dev * SUB + within, 0)
    local_cols = jax.random.randint(key_col, shape, lowest, GRID_ROWS * SUB)
    return ((segment * SUB + within).astype(jnp.int32), local_cols.astype(jnp.int32))


def draw_tile_rows(key, part):
    return place_tiles(key)[0]


def draw_tile_cols(key, part):
    return place_tiles(key)[1]


def draw_counts(key, part):
    key = jax.random.fold_in(key, 7)
    key_load, key_full = jax.random.split(key)
    level = jax.random.randint(key_load, (GRID_ROWS * GRID_COLS,), 1, 65)
    loads = jnp.maximum(1, TILES_DEV * level * level // 4096)
    fullest = jax.random.randint(key_full, (), 0, GRID_ROWS * GRID_COLS)
    loads = loads.at[fullest].set(TILES_DEV)
    return loads.reshape(GRID_ROWS, GRID_COLS).astype(jnp.int32)


def block_levels(stream_key, extent, pieces, low, top_value):
    gain = 1.0
    for dim, blocks in pieces:
        draws = jax.random.uniform(jax.random.fold_in(jax.random.fold_in(stream_key, 6), dim), (blocks,), jnp.float32, low / len(pieces), top_value / len(pieces))
        gain = gain * jnp.repeat(jnp.exp(draws), extent[dim] // blocks).reshape((-1,) + (1,) * (len(extent) - 1 - dim))
    return gain


def bell_draw(stream_key, dims, spread, reach, cuts=(), kind=jnp.bfloat16):
    drawn = jax.random.normal(stream_key, dims, jnp.float32) * spread
    if len(cuts) > 0:
        drawn = block_levels(stream_key, dims, cuts, -0.22, 0.18) * drawn
    return jnp.clip(drawn, min=-reach, max=reach).astype(kind)


def setup_inputs(seed: int = 0) -> dict:
    key_of = jax.random.split(jax.random.key(seed), 7)
    vectors = bell_draw(key_of[0], (NVEC, M), 1.0, 6.0, ((1, 256),))
    energies = jnp.clip(0.5 + 2.5 * jax.random.uniform(key_of[1], (M,), jnp.float32) ** block_levels(key_of[1], (M,), ((0, 256),), -0.2, 0.2), 0.5, 3.0)
    tiles = bell_draw(key_of[2], (GRID_ROWS, GRID_COLS, TILES_DEV, TILE, TILE), (TILES_DEV * TILE // (2 * SUB)) ** -0.5, 0.09375, ((0, 8), (1, 32)))
    tile_rows = draw_tile_rows(jax.random.fold_in(key_of[6], 71), 0)
    tile_cols = draw_tile_cols(jax.random.fold_in(key_of[6], 71), 0)
    counts = draw_counts(jax.random.fold_in(key_of[6], 71), 0)
    return {"vectors": vectors, "energies": energies, "tiles": tiles, "tile_rows": tile_rows, "tile_cols": tile_cols, "counts": counts}


def reference(vectors, energies, tiles, tile_rows, tile_cols, counts):
    nblk = M // TILE
    blocks = vectors.astype(jnp.float32).reshape(NVEC, nblk, TILE).transpose(1, 0, 2)
    ndev = GRID_ROWS * GRID_COLS
    flat_tiles = tiles.reshape(ndev, TILES_DEV, TILE, TILE)
    flat_rows = tile_rows.reshape(ndev, TILES_DEV)
    flat_cols = tile_cols.reshape(ndev, TILES_DEV)
    flat_counts = counts.reshape(ndev)
    order = jnp.arange(ndev).astype(jnp.int32)

    def step(total, inputs):
        block_tiles, local_rows, local_cols, live_count, device = inputs
        row_dev = device // GRID_COLS
        col_dev = device % GRID_COLS
        global_rows = (local_rows // SUB) * GRID_ROWS * SUB + row_dev * SUB + local_rows % SUB
        global_cols = col_dev * GRID_ROWS * SUB + local_cols
        live = (jnp.arange(TILES_DEV).astype(jnp.int32) < live_count)[:, None, None]
        tile_float = block_tiles.astype(jnp.float32)
        forward = jnp.einsum("tij,tvj->tvi", tile_float, blocks[global_cols])
        backward = jnp.einsum("tij,tvi->tvj", tile_float, blocks[global_rows])
        forward = jnp.where(live, forward, jnp.float32(0.0))
        backward = jnp.where(live, backward, jnp.float32(0.0))
        total = total + jax.ops.segment_sum(forward, global_rows, nblk)
        total = total + jax.ops.segment_sum(backward, global_cols, nblk)
        return total, None

    start = jnp.zeros((nblk, NVEC, TILE), jnp.float32)
    total, _ = lax.scan(step, start, (flat_tiles, flat_rows, flat_cols, flat_counts, order))
    result = total.transpose(1, 0, 2).reshape(NVEC, M) + energies[None, :] * vectors.astype(jnp.float32)
    return result.astype(jnp.bfloat16)
```

```python
import functools

import jax
import jax.numpy as jnp
from jax import lax
from jax.experimental import pallas as pl
from jax.experimental.pallas import tpu as pltpu
from jax.sharding import PartitionSpec as P

MESH = pl.DeviceIdType.MESH
NT = (((1,), (1,)), ((), ()))
NN = (((1,), (0,)), ((), ()))
BF, F32 = jnp.bfloat16, jnp.float32
LEVEL = 9
GROUP = 32


def remote(src, dst, send, recv, row, col):
    return pltpu.make_async_remote_copy(
        src_ref=src, dst_ref=dst, send_sem=send, recv_sem=recv,
        device_id=(row, col), device_id_type=MESH,
    )


def loop(lo, hi, step):
    lax.fori_loop(lo, hi, lambda i, c: (step(i), c)[1], 0)


def two_terms(x0, x1, t0, t1, forward):
    zero = jnp.zeros_like(x0)
    left = jnp.concatenate([x0, zero], 0).astype(BF)
    right = jnp.concatenate([zero, x1], 0).astype(BF)
    both = jnp.concatenate([left, right], 1)
    pair = jnp.concatenate([t0, t1], 1 if forward else 0)
    return lax.dot_general(both, pair, NT if forward else NN, preferred_element_type=F32)


def collect(picks, terms, slots, nvec, width, store):
    for v in range(nvec):
        term = terms[pl.ds(v, slots, stride=nvec), :]
        high = term.astype(BF)
        low = (term - high.astype(F32)).astype(BF)
        out = jnp.dot(picks, jnp.concatenate([high, low], 1), preferred_element_type=F32)
        store(v, out[:, :width] + out[:, width:])


def kernel(
    nrow, ncol,
    vec, en, tiles, rows, cols, cnt, out,
    tv, vbuf, ebuf, rows_s, rows_v, cols_s, cols_v, cnt_s,
    seg, segf, slab, slabf, terms, mine, other, partner, rsum, csum, crecv,
    tile_sem, in_sem, seg_send, seg_recv, slab_send, slab_recv,
    pair_send, pair_recv, rs_send, rs_recv, cs_send, cs_recv,
):
    slots, width = tv.shape[0], tv.shape[2]
    nvec = vec.shape[0]
    sub = vec.shape[1] // width
    nchip = ncol // 2
    r, c = lax.axis_index("row"), lax.axis_index("col")
    chip, core = c // 2, c % 2

    def chip_at(d):
        return lax.rem(chip + d, nchip)

    def row_at(d):
        return lax.rem(r + d, nrow)

    nch = slots // GROUP
    def tile_copy(g):
        part = pl.ds(pl.multiple_of(g * GROUP, GROUP), GROUP)
        return pltpu.make_async_copy(tiles.at[0, 0, part], tv.at[part], tile_sem.at[g])
    small = [
        pltpu.make_async_copy(s, d, in_sem.at[k])
        for k, (s, d) in enumerate((
            (vec, vbuf), (cols.at[0], cols_s), (rows.at[0], rows_s),
            (cols.at[0], cols_v), (rows.at[0], rows_v), (cnt, cnt_s), (en, ebuf),
        ))
    ]
    for copy in small:
        copy.start()
    loop(0, nch, lambda g: tile_copy(g).start())

    barrier = pltpu.get_barrier_semaphore()
    def greet(row, col):
        pl.semaphore_signal(barrier, inc=1, device_id=(row, col), device_id_type=MESH)
    greet(r, chip * 2 + 1 - core)
    loop(1, nrow, lambda d: greet(row_at(d), c))
    loop(1, nchip, lambda d: greet(r, chip_at(d) * 2 + core))

    for copy in small:
        copy.wait()
    own = jnp.concatenate(
        [vbuf[:, s * width:(s + 1) * width].astype(F32) for s in range(sub)], 0
    )
    seg[r] = own.astype(BF)
    slab[core, chip] = own.astype(BF)
    pl.semaphore_wait(barrier, nrow + nchip - 1)

    def seg_copy(d):
        return remote(seg.at[r], seg.at[r], seg_send.at[d], seg_recv.at[d], row_at(d), c)
    def slab_copy(d):
        return remote(slab.at[core, chip], slab.at[core, chip], slab_send.at[d], slab_recv.at[d],
                      r, chip_at(d) * 2 + core)
    if LEVEL >= 2:
        loop(1, nrow, lambda d: seg_copy(d).start())
        loop(1, nchip, lambda d: slab_copy(d).start())

    live = lax.broadcasted_iota(jnp.int32, (1, slots), 1) < cnt_s[0, 0]
    a, b = rows_v[...], cols_v[...]
    place = (a // sub % 2) * (nchip * sub) + (a // (2 * sub)) * sub + a % sub
    place = jnp.where(live, place, -1)
    b = jnp.where(live, b, -1)

    def picks(targets, first, count):
        index = lax.broadcasted_iota(jnp.int32, (count, slots), 0) + first
        return (index == targets).astype(BF)

    pair_slab = remote(slab.at[core], slab.at[core], pair_send.at[0], pair_recv.at[0],
                       r, chip * 2 + 1 - core)
    pair_sum = remote(other, partner, pair_send.at[1], pair_recv.at[1], r, chip * 2 + 1 - core)
    nb = nrow * sub

    if LEVEL >= 2:
        loop(1, nrow, lambda d: seg_copy(d).wait_recv())
        for k in range(nrow):
            block = seg[k].astype(F32)
            for s in range(sub):
                segf[k * sub + s] = block[s * nvec:(s + 1) * nvec]

    def forward(g):
        tile_copy(g).wait()
        for u in range(0, GROUP, 2):
            t = g * GROUP + u
            terms[pl.ds(pl.multiple_of(t * nvec, 2 * nvec), 2 * nvec), :] = two_terms(
                segf[cols_s[0, t]], segf[cols_s[0, t + 1]], tv[t], tv[t + 1], True)
        @pl.when(g == nch // 2)
        def _():
            loop(1, nchip, lambda d: slab_copy(d).wait_recv())
            pair_slab.start()

    def backward(g):
        for u in range(0, GROUP, 2):
            t = g * GROUP + u
            terms[pl.ds(pl.multiple_of(t * nvec, 2 * nvec), 2 * nvec), :] = two_terms(
                slabf[rows_s[0, t]], slabf[rows_s[0, t + 1]], tv[t], tv[t + 1], False)

    half = nchip * sub
    if LEVEL >= 3:
        loop(0, nch, forward)
    if LEVEL >= 4:
        def keep(ref):
            def store(v, x):
                ref[pl.ds(v, half, stride=nvec), :] = x
            return store
        collect(picks(place, (1 - core) * half, half), terms, slots, nvec, width, keep(other))
        pair_sum.start()
        collect(picks(place, core * half, half), terms, slots, nvec, width, keep(mine))

    size = sub * nvec
    def rs_copy(d):
        there = pl.ds(pl.multiple_of(chip_at(d) * size, size), size)
        return remote(mine.at[there], rsum.at[d], rs_send.at[d], rs_recv.at[d],
                      r, chip_at(d) * 2 + core)
    if LEVEL >= 5:
        pair_slab.wait_recv()
        for k in range(nchip):
            for m in range(2):
                block = slab[m, k].astype(F32)
                for s in range(sub):
                    slabf[(k * 2 + m) * sub + s] = block[s * nvec:(s + 1) * nvec]
        loop(0, nch // 4, backward)
        pair_sum.wait_recv()
        mine[...] += partner[...]
        loop(1, nchip, lambda d: rs_copy(d).start())
    if LEVEL >= 6:
        loop(nch // 4, nch, backward)
        def keep_cols(v, x):
            csum[pl.ds(v, nb, stride=nvec), :] = x
        collect(picks(b, 0, nb), terms, slots, nvec, width, keep_cols)
    def cs_copy(d):
        there = pl.ds(pl.multiple_of(row_at(d) * size, size), size)
        return remote(csum.at[there], crecv.at[d], cs_send.at[d], cs_recv.at[d], row_at(d), c)
    if LEVEL >= 7:
        loop(1, nrow, lambda d: cs_copy(d).start())

    total = own
    if LEVEL >= 6:
        total = jnp.concatenate(
            [own[s * nvec:(s + 1) * nvec] * ebuf[:, s * width:(s + 1) * width] for s in range(sub)], 0)
    if LEVEL >= 5:
        total = total + mine[pl.ds(pl.multiple_of(chip * size, size), size), :]
        loop(1, nchip, lambda d: rs_copy(d).wait_recv())
        for d in range(1, nchip):
            total = total + rsum[d]
    if LEVEL >= 7:
        total = total + csum[pl.ds(pl.multiple_of(r * size, size), size), :]
        loop(1, nrow, lambda d: cs_copy(d).wait_recv())
        for d in range(1, nrow):
            total = total + crecv[d]
    for s in range(sub):
        out[:, s * width:(s + 1) * width] = total[s * nvec:(s + 1) * nvec].astype(BF)

    if LEVEL >= 2:
        loop(1, nrow, lambda d: seg_copy(d).wait_send())
        loop(1, nchip, lambda d: slab_copy(d).wait_send())
    if LEVEL == 2:
        loop(1, nchip, lambda d: slab_copy(d).wait_recv())
    if LEVEL < 3:
        loop(0, nch, lambda g: tile_copy(g).wait())
    if LEVEL >= 3:
        pair_slab.wait_send()
        if LEVEL < 5:
            pair_slab.wait_recv()
    if LEVEL >= 4:
        pair_sum.wait_send()
        if LEVEL < 5:
            pair_sum.wait_recv()
    if LEVEL >= 5:
        loop(1, nchip, lambda d: rs_copy(d).wait_send())
    if LEVEL >= 7:
        loop(1, nrow, lambda d: cs_copy(d).wait_send())


def body(vectors, energies, tiles, tile_rows, tile_cols, counts):
    nrow, ncol = lax.axis_size("row"), lax.axis_size("col")
    slots, width = tiles.shape[2], tiles.shape[3]
    nvec, own = vectors.shape
    sub = own // width
    nchip = ncol // 2
    any_, dma = pl.BlockSpec(memory_space=pl.ANY), pltpu.SemaphoreType.DMA
    return pl.pallas_call(
        functools.partial(kernel, nrow, ncol),
        out_shape=jax.ShapeDtypeStruct(vectors.shape, BF),
        in_specs=[any_] * 6,
        out_specs=pl.BlockSpec(memory_space=pltpu.VMEM),
        scratch_shapes=[
            pltpu.VMEM((slots, width, width), BF),
            pltpu.VMEM((nvec, own), BF),
            pltpu.VMEM((1, own), F32),
            pltpu.SMEM((1, slots), jnp.int32),
            pltpu.VMEM((1, slots), jnp.int32),
            pltpu.SMEM((1, slots), jnp.int32),
            pltpu.VMEM((1, slots), jnp.int32),
            pltpu.SMEM((1, 1), jnp.int32),
            pltpu.VMEM((nrow, sub * nvec, width), BF),
            pltpu.VMEM((nrow * sub, nvec, width), F32),
            pltpu.VMEM((2, nchip, sub * nvec, width), BF),
            pltpu.VMEM((ncol * sub, nvec, width), F32),
            pltpu.VMEM((slots * nvec, width), F32),
            pltpu.VMEM((nchip * sub * nvec, width), F32),
            pltpu.VMEM((nchip * sub * nvec, width), F32),
            pltpu.VMEM((nchip * sub * nvec, width), F32),
            pltpu.VMEM((nchip, sub * nvec, width), F32),
            pltpu.VMEM((nrow * sub * nvec, width), F32),
            pltpu.VMEM((nrow, sub * nvec, width), F32),
            dma((slots // GROUP,)), dma((7,)),
            dma((nrow,)), dma((nrow,)), dma((nchip,)), dma((nchip,)),
            dma((2,)), dma((2,)), dma((nchip,)), dma((nchip,)), dma((nrow,)), dma((nrow,)),
        ],
        compiler_params=pltpu.CompilerParams(
            collective_id=0, has_side_effects=True, vmem_limit_bytes=56 * 2**20
        ),
    )(vectors, energies.reshape(1, own), tiles, tile_rows, tile_cols, counts)


def solution(mesh):
    placed = (
        P(None, ("col", "row")),
        P(("col", "row")),
        P("row", "col", None, None, None),
        P("row", "col", None),
        P("row", "col", None),
        P("row", "col"),
    )
    return jax.shard_map(
        body, mesh=mesh, in_specs=placed, out_specs=P(None, ("col", "row")), check_vma=False
    )
```

```python
import functools

import jax
import jax.numpy as jnp
from jax import lax
from jax.experimental import pallas as pl
from jax.experimental.pallas import tpu as pltpu
from jax.sharding import PartitionSpec as P

MESH = pl.DeviceIdType.MESH
NT = (((1,), (1,)), ((), ()))
NN = (((1,), (0,)), ((), ()))
BF, F32 = jnp.bfloat16, jnp.float32
GROUP = 128
PIECES = 4


def remote(src, dst, send, recv, row, col):
    return pltpu.make_async_remote_copy(
        src_ref=src, dst_ref=dst, send_sem=send, recv_sem=recv,
        device_id=(row, col), device_id_type=MESH,
    )


def loop(lo, hi, step):
    lax.fori_loop(lo, hi, lambda i, c: (step(i), c)[1], 0)


def two_terms(x0, x1, t0, t1, forward):
    zero = jnp.zeros_like(x0)
    left = jnp.concatenate([x0, zero], 0).astype(BF)
    right = jnp.concatenate([zero, x1], 0).astype(BF)
    both = jnp.concatenate([left, right], 1)
    pair = jnp.concatenate([t0, t1], 1 if forward else 0)
    return lax.dot_general(both, pair, NT if forward else NN, preferred_element_type=F32)


def collect(picks, terms, slots, nvec, width, store):
    for v in range(nvec):
        term = terms[pl.ds(v, slots, stride=nvec), :]
        high = term.astype(BF)
        low = (term - high.astype(F32)).astype(BF)
        out = jnp.dot(picks, jnp.concatenate([high, low], 1), preferred_element_type=F32)
        store(v, out[:, :width] + out[:, width:])


def kernel(
    nrow, ncol,
    vec, en, tiles, rows, cols, cnt, out,
    tv, vbuf, ebuf, rows_s, rows_v, cols_s, cols_v, cnt_s,
    seg, segf, slab, slabf, terms, mine, other, partner, rsum, csum, crecv,
    tile_sem, in_sem, seg_send, seg_recv, slab_send, slab_recv,
    pair_send, pair_recv, rs_send, rs_recv, cs_send, cs_recv, ready,
):
    slots, width = tv.shape[0], tv.shape[2]
    nvec = vec.shape[0]
    sub = vec.shape[1] // width
    nchip = ncol // 2
    r, c = lax.axis_index("row"), lax.axis_index("col")
    chip, core = c // 2, c % 2

    def row_at(d):
        return lax.rem(r + d, nrow)

    split = nchip // 2
    barrier = pltpu.get_barrier_semaphore()
    def greet(row, col):
        pl.semaphore_signal(barrier, inc=1, device_id=(row, col), device_id_type=MESH)
    greet(r, chip * 2 + 1 - core)
    loop(1, nrow, lambda d: greet(row_at(d), c))
    loop(chip + 1, nchip, lambda k: greet(r, k * 2 + core))
    @pl.when(chip < split)
    def _():
        loop(0, chip, lambda k: greet(r, k * 2 + core))

    nch = slots // GROUP
    def tile_copy(g):
        part = pl.ds(pl.multiple_of(g * GROUP, GROUP), GROUP)
        return pltpu.make_async_copy(tiles.at[0, 0, part], tv.at[part], tile_sem.at[g])
    small = [
        pltpu.make_async_copy(s, d, in_sem.at[k])
        for k, (s, d) in enumerate((
            (vec, vbuf), (cols.at[0], cols_s), (rows.at[0], rows_s),
            (cols.at[0], cols_v), (rows.at[0], rows_v), (cnt, cnt_s), (en, ebuf),
        ))
    ]
    for copy in small:
        copy.start()
    loop(0, nch, lambda g: tile_copy(g).start())

    for copy in small:
        copy.wait()
    own = jnp.concatenate(
        [vbuf[:, s * width:(s + 1) * width].astype(F32) for s in range(sub)], 0
    )
    seg[r] = own.astype(BF)
    slab[core, chip] = own.astype(BF)

    live = lax.broadcasted_iota(jnp.int32, (1, slots), 1) < cnt_s[0, 0]
    a, b = rows_v[...], cols_v[...]
    place = (a // sub % 2) * (nchip * sub) + (a // (2 * sub)) * sub + a % sub
    place = jnp.where(live, place, -1)
    b = jnp.where(live, b, -1)

    def picks(targets, first, count):
        index = lax.broadcasted_iota(jnp.int32, (count, slots), 0) + first
        return (index == targets).astype(BF)

    near = chip < split
    pl.semaphore_wait(barrier, nrow + jnp.where(near, split - 1, chip))

    def seg_copy(d):
        return remote(seg.at[r], seg.at[r], seg_send.at[d], seg_recv.at[d], row_at(d), c)
    def slab_out(k):
        return remote(slab.at[core, chip], slab.at[core, chip], slab_send.at[k], slab_recv.at[chip],
                      r, k * 2 + core)
    def slab_in(k):
        return remote(slab.at[core, k], slab.at[core, k], slab_send.at[k], slab_recv.at[k],
                      r, k * 2 + core)
    loop(1, nrow, lambda d: seg_copy(d).start())
    first_far = jnp.maximum(chip + 1, split)
    loop(chip + 1, split, lambda k: slab_out(k).start())
    @pl.when(jnp.logical_not(near))
    def _():
        loop(0, chip, lambda k: pl.semaphore_signal(
            ready.at[chip], inc=1, device_id=(r, k * 2 + core), device_id_type=MESH))

    pair_slab = remote(slab.at[core], slab.at[core], pair_send.at[0], pair_recv.at[0],
                       r, chip * 2 + 1 - core)
    nb = nrow * sub
    size = sub * nvec
    piece = nchip // PIECES

    loop(1, nrow, lambda d: seg_copy(d).wait_recv())
    for k in range(nrow):
        block = seg[k].astype(F32)
        for s in range(sub):
            segf[k * sub + s] = block[s * nvec:(s + 1) * nvec]

    def relay():
        loop(0, chip, lambda k: slab_in(k).wait_recv())
        pair_slab.start()

    def to_far(k):
        pl.semaphore_wait(ready.at[k], 1)
        slab_out(k).start()

    def forward(g):
        @pl.when(g == nch // 2)
        def _():
            pl.when(near)(relay)
            loop(first_far, nchip, to_far)
        tile_copy(g).wait()
        for u in range(0, GROUP, 2):
            t = g * GROUP + u
            terms[pl.ds(pl.multiple_of(t * nvec, 2 * nvec), 2 * nvec), :] = two_terms(
                segf[cols_s[0, t]], segf[cols_s[0, t + 1]], tv[t], tv[t + 1], True)

    loop(0, nch, forward)

    half = nchip * sub
    def keep(ref):
        def store(v, x):
            ref[pl.ds(v, half, stride=nvec), :] = x
        return store

    def pair_sum(q):
        part = pl.ds(pl.multiple_of(q * piece * size, piece * size), piece * size)
        return remote(other.at[part], partner.at[part], pair_send.at[1 + q], pair_recv.at[1 + q],
                      r, chip * 2 + 1 - core)
    npiece = chip // piece + 1
    collect(picks(place, (1 - core) * half, half), terms, slots, nvec, width, keep(other))
    loop(0, npiece, lambda q: pair_sum(q).start())
    collect(picks(place, core * half, half), terms, slots, nvec, width, keep(mine))

    def rs_out(k):
        there = pl.ds(pl.multiple_of(k * size, size), size)
        return remote(mine.at[there], rsum.at[chip], rs_send.at[k], rs_recv.at[chip], r, k * 2 + core)
    def rs_in(k):
        return remote(rsum.at[k], rsum.at[k], rs_send.at[k], rs_recv.at[k], r, k * 2 + core)

    def send_rows():
        def one(q):
            pair_sum(q).wait_recv()
            part = pl.ds(pl.multiple_of(q * piece * size, piece * size), piece * size)
            mine[part, :] += partner[part, :]
            loop(q * piece, jnp.minimum((q + 1) * piece, chip), lambda k: rs_out(k).start())
        loop(0, npiece, one)

    @pl.when(jnp.logical_not(near))
    def _():
        send_rows()
        relay()

    pair_slab.wait_recv()
    for k in range(nchip):
        for m in range(2):
            block = slab[m, k].astype(F32)
            for s in range(sub):
                slabf[(k * 2 + m) * sub + s] = block[s * nvec:(s + 1) * nvec]

    def backward(g):
        @pl.when(jnp.logical_and(near, g == nch // 2))
        def _():
            send_rows()
        for u in range(0, GROUP, 2):
            t = g * GROUP + u
            terms[pl.ds(pl.multiple_of(t * nvec, 2 * nvec), 2 * nvec), :] = two_terms(
                slabf[rows_s[0, t]], slabf[rows_s[0, t + 1]], tv[t], tv[t + 1], False)

    loop(0, nch, backward)
    def keep_cols(v, x):
        csum[pl.ds(v, nb, stride=nvec), :] = x
    collect(picks(b, 0, nb), terms, slots, nvec, width, keep_cols)
    def cs_copy(d):
        there = pl.ds(pl.multiple_of(row_at(d) * size, size), size)
        return remote(csum.at[there], crecv.at[d], cs_send.at[d], cs_recv.at[d], row_at(d), c)
    loop(1, nrow, lambda d: cs_copy(d).start())

    total = jnp.concatenate(
        [own[s * nvec:(s + 1) * nvec] * ebuf[:, s * width:(s + 1) * width] for s in range(sub)], 0)
    total = total + mine[pl.ds(pl.multiple_of(chip * size, size), size), :]
    total = total + csum[pl.ds(pl.multiple_of(r * size, size), size), :]
    def add_cols(d, x):
        cs_copy(d).wait_recv()
        return x + crecv[d]
    def add_rows(k, x):
        rs_in(k).wait_recv()
        return x + rsum[k]
    total = lax.fori_loop(1, nrow, add_cols, total)
    total = lax.fori_loop(chip + 1, nchip, add_rows, total)
    for s in range(sub):
        out[:, s * width:(s + 1) * width] = total[s * nvec:(s + 1) * nvec].astype(BF)

    loop(1, nrow, lambda d: seg_copy(d).wait_send())
    loop(chip + 1, nchip, lambda k: slab_out(k).wait_send())
    pair_slab.wait_send()
    loop(0, npiece, lambda q: pair_sum(q).wait_send())
    loop(0, chip, lambda k: rs_out(k).wait_send())
    loop(1, nrow, lambda d: cs_copy(d).wait_send())


def body(vectors, energies, tiles, tile_rows, tile_cols, counts):
    nrow, ncol = lax.axis_size("row"), lax.axis_size("col")
    slots, width = tiles.shape[2], tiles.shape[3]
    nvec, own = vectors.shape
    sub = own // width
    nchip = ncol // 2
    any_, dma = pl.BlockSpec(memory_space=pl.ANY), pltpu.SemaphoreType.DMA
    return pl.pallas_call(
        functools.partial(kernel, nrow, ncol),
        out_shape=pltpu.VMEM(vectors.shape, BF),
        in_specs=[any_] * 6,
        out_specs=pl.BlockSpec(memory_space=pltpu.VMEM),
        scratch_shapes=[
            pltpu.VMEM((slots, width, width), BF),
            pltpu.VMEM((nvec, own), BF),
            pltpu.VMEM((1, own), F32),
            pltpu.SMEM((1, slots), jnp.int32),
            pltpu.VMEM((1, slots), jnp.int32),
            pltpu.SMEM((1, slots), jnp.int32),
            pltpu.VMEM((1, slots), jnp.int32),
            pltpu.SMEM((1, 1), jnp.int32),
            pltpu.VMEM((nrow, sub * nvec, width), BF),
            pltpu.VMEM((nrow * sub, nvec, width), F32),
            pltpu.VMEM((2, nchip, sub * nvec, width), BF),
            pltpu.VMEM((ncol * sub, nvec, width), F32),
            pltpu.VMEM((slots * nvec, width), F32),
            pltpu.VMEM((nchip * sub * nvec, width), F32),
            pltpu.VMEM((nchip * sub * nvec, width), F32),
            pltpu.VMEM((nchip * sub * nvec, width), F32),
            pltpu.VMEM((nchip, sub * nvec, width), F32),
            pltpu.VMEM((nrow * sub * nvec, width), F32),
            pltpu.VMEM((nrow, sub * nvec, width), F32),
            dma((slots // GROUP,)), dma((7,)),
            dma((nrow,)), dma((nrow,)), dma((nchip,)), dma((nchip,)),
            dma((1 + PIECES,)), dma((1 + PIECES,)), dma((nchip,)), dma((nchip,)), dma((nrow,)), dma((nrow,)),
            pltpu.SemaphoreType.REGULAR((nchip,)),
        ],
        compiler_params=pltpu.CompilerParams(
            collective_id=0, has_side_effects=True, vmem_limit_bytes=56 * 2**20
        ),
    )(vectors, energies.reshape(1, own), tiles, tile_rows, tile_cols, counts)


def solution(mesh):
    placed = (
        P(None, ("col", "row")),
        P(("col", "row")),
        P("row", "col", None, None, None),
        P("row", "col", None),
        P("row", "col", None),
        P("row", "col"),
    )
    return jax.shard_map(
        body, mesh=mesh, in_specs=placed, out_specs=P(None, ("col", "row")), check_vma=False
    )
```

```python
import functools

import jax
import jax.numpy as jnp
from jax import lax
from jax.experimental import pallas as pl
from jax.experimental.pallas import tpu as pltpu
from jax.sharding import PartitionSpec as P

MESH = pl.DeviceIdType.MESH
BF, F32 = jnp.bfloat16, jnp.float32
GROUP = 128
EARLY = 8
TURN = 32
LIMIT = 32767.0
PIECES = 4


def remote(src, dst, send, recv, row, col):
    return pltpu.make_async_remote_copy(
        src_ref=src, dst_ref=dst, send_sem=send, recv_sem=recv,
        device_id=(row, col), device_id_type=MESH,
    )


def loop(lo, hi, step):
    lax.fori_loop(lo, hi, lambda i, c: (step(i), c)[1], 0)


def two_terms(x0, x1, t0, t1):
    zero = jnp.zeros_like(x0)
    left = jnp.concatenate([x0, zero], 0).astype(BF)
    right = jnp.concatenate([zero, x1], 0).astype(BF)
    both = jnp.concatenate([left, right], 1)
    return jnp.dot(both, jnp.concatenate([t0, t1], 0), preferred_element_type=F32)


def collect(picks, terms, slots, nvec, width, store):
    for v in range(nvec):
        term = terms[pl.ds(v, slots, stride=nvec), :]
        high = term.astype(BF)
        low = (term - high.astype(F32)).astype(BF)
        out = jnp.dot(picks, jnp.concatenate([high, low], 1), preferred_element_type=F32)
        store(v, out[:, :width] + out[:, width:])


def kernel(
    nrow, ncol,
    vec, en, tiles, rows, cols, cnt, out,
    tv, flip, vbuf, ebuf, rows_s, rows_v, cols_s, cols_v, cnt_s,
    seg, segf, slab, slabf, terms, mine, other, partner, fixed, scale, rsum, rscale, csum, crecv,
    tile_sem, in_sem, seg_send, seg_recv, slab_send, slab_recv,
    pair_send, pair_recv, rs_send, rs_recv, cs_send, cs_recv, ready,
):
    slots, width = tv.shape[0], tv.shape[2]
    nvec = vec.shape[0]
    sub = vec.shape[1] // width
    nchip = ncol // 2
    r, c = lax.axis_index("row"), lax.axis_index("col")
    chip, core = c // 2, c % 2

    def row_at(d):
        return lax.rem(r + d, nrow)

    barrier = pltpu.get_barrier_semaphore()
    def greet(row, col):
        pl.semaphore_signal(barrier, inc=1, device_id=(row, col), device_id_type=MESH)
    greet(r, chip * 2 + 1 - core)
    loop(1, nrow, lambda d: greet(row_at(d), c))
    loop(chip + 1, nchip, lambda k: greet(r, k * 2 + core))

    nch = slots // TURN
    def tile_copy(g):
        part = pl.ds(pl.multiple_of(g * TURN, TURN), TURN)
        return pltpu.make_async_copy(tiles.at[0, 0, part], tv.at[part], tile_sem.at[g])
    small = [
        pltpu.make_async_copy(s, d, in_sem.at[k])
        for k, (s, d) in enumerate((
            (vec, vbuf), (cols.at[0], cols_s), (rows.at[0], rows_s),
            (cols.at[0], cols_v), (rows.at[0], rows_v), (cnt, cnt_s), (en, ebuf),
        ))
    ]
    for copy in small:
        copy.start()
    loop(0, nch, lambda g: tile_copy(g).start())

    for copy in small:
        copy.wait()
    own = jnp.concatenate(
        [vbuf[:, s * width:(s + 1) * width].astype(F32) for s in range(sub)], 0
    )
    seg[r] = own.astype(BF)
    slab[core, chip] = own.astype(BF)

    live = lax.broadcasted_iota(jnp.int32, (1, slots), 1) < cnt_s[0, 0]
    a, b = rows_v[...], cols_v[...]
    place = (a // sub % 2) * (nchip * sub) + (a // (2 * sub)) * sub + a % sub
    place = jnp.where(live, place, -1)
    b = jnp.where(live, b, -1)

    def picks(targets, first, count):
        index = lax.broadcasted_iota(jnp.int32, (count, slots), 0) + first
        return (index == targets).astype(BF)

    pl.semaphore_wait(barrier, nrow + chip)

    def seg_copy(d):
        return remote(seg.at[r], seg.at[r], seg_send.at[d], seg_recv.at[d], row_at(d), c)
    def slab_out(k):
        return remote(slab.at[core, chip], slab.at[core, chip], slab_send.at[k], slab_recv.at[chip],
                      r, k * 2 + core)
    def slab_in(k):
        return remote(slab.at[core, k], slab.at[core, k], slab_send.at[k], slab_recv.at[k],
                      r, k * 2 + core)
    loop(1, nrow, lambda d: seg_copy(d).start())
    loop(0, chip, lambda k: pl.semaphore_signal(
        ready.at[chip], inc=1, device_id=(r, k * 2 + core), device_id_type=MESH))

    def turn(g):
        tile_copy(g).wait()
        for u in range(TURN):
            flip[g * TURN + u] = tv[g * TURN + u].T
    loop(0, nch, turn)

    pair_slab = remote(slab.at[core], slab.at[core], pair_send.at[0], pair_recv.at[0],
                       r, chip * 2 + 1 - core)
    nb = nrow * sub
    size = sub * nvec
    piece = nchip // PIECES

    loop(1, nrow, lambda d: seg_copy(d).wait_recv())
    for k in range(nrow):
        block = seg[k].astype(F32)
        for s in range(sub):
            segf[k * sub + s] = block[s * nvec:(s + 1) * nvec]

    def relay():
        loop(0, chip, lambda k: slab_in(k).wait_recv())
        pair_slab.start()

    def to_later(k):
        pl.semaphore_wait(ready.at[k], 1)
        slab_out(k).start()

    def products(source, index, matrix):
        def step(g):
            for u in range(0, GROUP, 2):
                t = g * GROUP + u
                terms[pl.ds(pl.multiple_of(t * nvec, 2 * nvec), 2 * nvec), :] = two_terms(
                    source[index[0, t]], source[index[0, t + 1]], matrix[t], matrix[t + 1])
        loop(0, slots // GROUP, step)

    early = chip < max(nchip // EARLY, 1)
    first = chip < max(nchip // 8, 1)
    split = nchip // 2
    @pl.when(jnp.logical_not(early))
    def _():
        loop(chip + 1, nchip, to_later)
    products(segf, cols_s, flip)

    half = nchip * sub
    def keep(ref):
        def store(v, x):
            ref[pl.ds(v, half, stride=nvec), :] = x
        return store

    def pair_sum(q):
        part = pl.ds(pl.multiple_of(q * piece * size, piece * size), piece * size)
        return remote(other.at[part], partner.at[part], pair_send.at[1 + q], pair_recv.at[1 + q],
                      r, chip * 2 + 1 - core)
    npiece = chip // piece + 1
    collect(picks(place, (1 - core) * half, half), terms, slots, nvec, width, keep(other))
    loop(0, npiece, lambda q: pair_sum(q).start())
    collect(picks(place, core * half, half), terms, slots, nvec, width, keep(mine))

    def rs_out(k):
        to = (r, k * 2 + core)
        return (remote(fixed.at[k], rsum.at[chip], rs_send.at[0, k], rs_recv.at[0, chip], *to),
                remote(scale.at[k], rscale.at[chip], rs_send.at[1, k], rs_recv.at[1, chip], *to))
    def rs_in(k):
        to = (r, k * 2 + core)
        return (remote(rsum.at[k], rsum.at[k], rs_send.at[0, k], rs_recv.at[0, k], *to),
                remote(rscale.at[k], rscale.at[k], rs_send.at[1, k], rs_recv.at[1, k], *to))
    def rs_start(k):
        for copy in rs_out(k):
            copy.start()
    def rs_wait(k):
        for copy in rs_out(k):
            copy.wait_send()

    def send_rows(q):
        pair_sum(q).wait_recv()
        for u in range(piece):
            k = q * piece + u
            part = pl.ds(pl.multiple_of(k * size, size), size)
            x = mine[part, :] + partner[part, :]
            mine[part, :] = x
            most = jnp.max(jnp.abs(x), axis=0, keepdims=True)
            some = most > 1e-30
            fixed[k] = jnp.round(x * jnp.where(some, LIMIT / jnp.where(some, most, 1.0), 0.0)).astype(jnp.int32).astype(jnp.int16)
            scale[k] = most * (1.0 / LIMIT)
        loop(q * piece, jnp.minimum((q + 1) * piece, chip), rs_start)
    loop(0, npiece, send_rows)

    @pl.when(early)
    def _():
        loop(chip + 1, split, to_later)
        pl.when(first)(relay)
        loop(split, nchip, to_later)
    pl.when(jnp.logical_not(first))(relay)

    pair_slab.wait_recv()
    for k in range(nchip):
        for m in range(2):
            block = slab[m, k].astype(F32)
            for s in range(sub):
                slabf[(k * 2 + m) * sub + s] = block[s * nvec:(s + 1) * nvec]

    products(slabf, rows_s, tv)
    def keep_cols(v, x):
        csum[pl.ds(v, nb, stride=nvec), :] = x
    collect(picks(b, 0, nb), terms, slots, nvec, width, keep_cols)
    def cs_copy(d):
        there = pl.ds(pl.multiple_of(row_at(d) * size, size), size)
        return remote(csum.at[there], crecv.at[d], cs_send.at[d], cs_recv.at[d], row_at(d), c)
    loop(1, nrow, lambda d: cs_copy(d).start())

    total = jnp.concatenate(
        [own[s * nvec:(s + 1) * nvec] * ebuf[:, s * width:(s + 1) * width] for s in range(sub)], 0)
    total = total + mine[pl.ds(pl.multiple_of(chip * size, size), size), :]
    total = total + csum[pl.ds(pl.multiple_of(r * size, size), size), :]
    def add_cols(d, x):
        cs_copy(d).wait_recv()
        return x + crecv[d]
    def add_rows(k, x):
        for copy in rs_in(k):
            copy.wait_recv()
        return x + rsum[k].astype(jnp.int32).astype(F32) * rscale[k]
    total = lax.fori_loop(1, nrow, add_cols, total)
    total = lax.fori_loop(chip + 1, nchip, add_rows, total)
    for s in range(sub):
        out[:, s * width:(s + 1) * width] = total[s * nvec:(s + 1) * nvec].astype(BF)

    loop(1, nrow, lambda d: seg_copy(d).wait_send())
    loop(chip + 1, nchip, lambda k: slab_out(k).wait_send())
    pair_slab.wait_send()
    loop(0, npiece, lambda q: pair_sum(q).wait_send())
    loop(0, chip, rs_wait)
    loop(1, nrow, lambda d: cs_copy(d).wait_send())


def body(vectors, energies, tiles, tile_rows, tile_cols, counts):
    nrow, ncol = lax.axis_size("row"), lax.axis_size("col")
    slots, width = tiles.shape[2], tiles.shape[3]
    nvec, own = vectors.shape
    sub = own // width
    nchip = ncol // 2
    any_, dma = pl.BlockSpec(memory_space=pl.ANY), pltpu.SemaphoreType.DMA
    return pl.pallas_call(
        functools.partial(kernel, nrow, ncol),
        out_shape=pltpu.VMEM(vectors.shape, BF),
        in_specs=[any_] * 6,
        out_specs=pl.BlockSpec(memory_space=pltpu.VMEM),
        scratch_shapes=[
            pltpu.VMEM((slots, width, width), BF),
            pltpu.VMEM((slots, width, width), BF),
            pltpu.VMEM((nvec, own), BF),
            pltpu.VMEM((1, own), F32),
            pltpu.SMEM((1, slots), jnp.int32),
            pltpu.VMEM((1, slots), jnp.int32),
            pltpu.SMEM((1, slots), jnp.int32),
            pltpu.VMEM((1, slots), jnp.int32),
            pltpu.SMEM((1, 1), jnp.int32),
            pltpu.VMEM((nrow, sub * nvec, width), BF),
            pltpu.VMEM((nrow * sub, nvec, width), F32),
            pltpu.VMEM((2, nchip, sub * nvec, width), BF),
            pltpu.VMEM((ncol * sub, nvec, width), F32),
            pltpu.VMEM((slots * nvec, width), F32),
            pltpu.VMEM((nchip * sub * nvec, width), F32),
            pltpu.VMEM((nchip * sub * nvec, width), F32),
            pltpu.VMEM((nchip * sub * nvec, width), F32),
            pltpu.VMEM((nchip, sub * nvec, width), jnp.int16),
            pltpu.VMEM((nchip, 1, width), F32),
            pltpu.VMEM((nchip, sub * nvec, width), jnp.int16),
            pltpu.VMEM((nchip, 1, width), F32),
            pltpu.VMEM((nrow * sub * nvec, width), F32),
            pltpu.VMEM((nrow, sub * nvec, width), F32),
            dma((slots // TURN,)), dma((7,)),
            dma((nrow,)), dma((nrow,)), dma((nchip,)), dma((nchip,)),
            dma((1 + PIECES,)), dma((1 + PIECES,)), dma((2, nchip)), dma((2, nchip)), dma((nrow,)), dma((nrow,)),
            pltpu.SemaphoreType.REGULAR((nchip,)),
        ],
        compiler_params=pltpu.CompilerParams(
            collective_id=0, has_side_effects=True, vmem_limit_bytes=56 * 2**20
        ),
    )(vectors, energies.reshape(1, own), tiles, tile_rows, tile_cols, counts)


def solution(mesh):
    placed = (
        P(None, ("col", "row")),
        P(("col", "row")),
        P("row", "col", None, None, None),
        P("row", "col", None),
        P("row", "col", None),
        P("row", "col"),
    )
    return jax.shard_map(
        body, mesh=mesh, in_specs=placed, out_specs=P(None, ("col", "row")), check_vma=False
    )
```

```python
import functools

import jax
import jax.numpy as jnp
from jax import lax
from jax.experimental import pallas as pl
from jax.experimental.pallas import tpu as pltpu
from jax.sharding import PartitionSpec as P

MESH = pl.DeviceIdType.MESH
BF, F32 = jnp.bfloat16, jnp.float32
GROUP = 256
AHEAD = 8
TURN = 32
LIMIT = 32766.0
PIECES = 4


def remote(src, dst, send, recv, row, col):
    return pltpu.make_async_remote_copy(
        src_ref=src, dst_ref=dst, send_sem=send, recv_sem=recv,
        device_id=(row, col), device_id_type=MESH,
    )


def loop(lo, hi, step):
    lax.fori_loop(lo, hi, lambda i, c: (step(i), c)[1], 0)


def two_terms(x0, x1, t0, t1):
    zero = jnp.zeros_like(x0)
    left = jnp.concatenate([x0, zero], 0).astype(BF)
    right = jnp.concatenate([zero, x1], 0).astype(BF)
    both = jnp.concatenate([left, right], 1)
    return jnp.dot(both, jnp.concatenate([t0, t1], 0), preferred_element_type=F32)


def collect(picks, terms, slots, nvec, width, store):
    for v in range(nvec):
        term = terms[pl.ds(v, slots, stride=nvec), :]
        high = term.astype(BF)
        low = (term - high.astype(F32)).astype(BF)
        out = jnp.dot(picks, jnp.concatenate([high, low], 1), preferred_element_type=F32)
        store(v, out[:, :width] + out[:, width:])


def kernel(
    nrow, ncol,
    vec, en, tiles, rows, cols, cnt, out,
    tv, flip, vbuf, ebuf, rows_s, rows_v, cols_s, cols_v, cnt_s,
    seg, segf, slab, slabf, terms, mine, other, partner, fixed, rsum, csum, cfixed, crecv,
    tile_sem, in_sem, seg_send, seg_recv, slab_send, slab_recv,
    pair_send, pair_recv, rs_send, rs_recv, cs_send, cs_recv, ready,
):
    slots, width = tv.shape[0], tv.shape[2]
    nvec = vec.shape[0]
    sub = vec.shape[1] // width
    nchip = ncol // 2
    r, c = lax.axis_index("row"), lax.axis_index("col")
    chip, core = c // 2, c % 2

    def row_at(d):
        return lax.rem(r + d, nrow)

    barrier = pltpu.get_barrier_semaphore()
    def greet(row, col):
        pl.semaphore_signal(barrier, inc=1, device_id=(row, col), device_id_type=MESH)
    greet(r, chip * 2 + 1 - core)
    loop(1, nrow, lambda d: greet(row_at(d), c))
    loop(chip + 1, nchip, lambda k: greet(r, k * 2 + core))

    nch = slots // TURN
    def tile_copy(g):
        part = pl.ds(pl.multiple_of(g * TURN, TURN), TURN)
        return pltpu.make_async_copy(tiles.at[0, 0, part], tv.at[part], tile_sem.at[g])
    small = [
        pltpu.make_async_copy(s, d, in_sem.at[k])
        for k, (s, d) in enumerate((
            (vec, vbuf), (cols.at[0], cols_s), (rows.at[0], rows_s),
            (cols.at[0], cols_v), (rows.at[0], rows_v), (cnt, cnt_s), (en, ebuf),
        ))
    ]
    for copy in small:
        copy.start()
    loop(0, nch, lambda g: tile_copy(g).start())

    for copy in small:
        copy.wait()
    own = jnp.concatenate(
        [vbuf[:, s * width:(s + 1) * width].astype(F32) for s in range(sub)], 0
    )
    seg[r] = own.astype(BF)
    slab[core, chip] = own.astype(BF)

    live = lax.broadcasted_iota(jnp.int32, (1, slots), 1) < cnt_s[0, 0]
    a, b = rows_v[...], cols_v[...]
    place = (a // sub % 2) * (nchip * sub) + (a // (2 * sub)) * sub + a % sub
    place = jnp.where(live, place, -1)
    b = jnp.where(live, b, -1)

    def picks(targets, first, count):
        index = lax.broadcasted_iota(jnp.int32, (count, slots), 0) + first
        return (index == targets).astype(BF)

    def turn(g):
        tile_copy(g).wait()
        for u in range(TURN):
            flip[g * TURN + u] = tv[g * TURN + u].T
    def turn_all():
        loop(0, nch, turn)
    split = nchip // 2
    pl.semaphore_wait(barrier, nrow + chip)

    def seg_copy(d):
        return remote(seg.at[r], seg.at[r], seg_send.at[d], seg_recv.at[d], row_at(d), c)
    def slab_out(k):
        return remote(slab.at[core, chip], slab.at[core, chip], slab_send.at[k], slab_recv.at[chip],
                      r, k * 2 + core)
    def slab_in(k):
        return remote(slab.at[core, k], slab.at[core, k], slab_send.at[k], slab_recv.at[k],
                      r, k * 2 + core)
    loop(1, nrow, lambda d: seg_copy(d).start())
    loop(0, chip, lambda k: pl.semaphore_signal(
        ready.at[chip], inc=1, device_id=(r, k * 2 + core), device_id_type=MESH))

    turn_all()

    pair_slab = remote(slab.at[core], slab.at[core], pair_send.at[0], pair_recv.at[0],
                       r, chip * 2 + 1 - core)
    nb = nrow * sub
    size = sub * nvec
    piece = nchip // PIECES

    def relay():
        loop(0, chip, lambda k: slab_in(k).wait_recv())
        pair_slab.start()

    def to_later(k):
        pl.semaphore_wait(ready.at[k], 1)
        slab_out(k).start()

    first = chip < max(nchip // 8, 1)
    close = jnp.where(chip < split, jnp.where(first, split, nchip), jnp.minimum(chip // 2 * 2 + AHEAD, nchip))
    loop(chip + 1, close, to_later)

    loop(1, nrow, lambda d: seg_copy(d).wait_recv())
    for k in range(nrow):
        block = seg[k].astype(F32)
        for s in range(sub):
            segf[k * sub + s] = block[s * nvec:(s + 1) * nvec]

    def products(source, index, matrix):
        def step(g):
            for u in range(0, GROUP, 2):
                t = g * GROUP + u
                terms[pl.ds(pl.multiple_of(t * nvec, 2 * nvec), 2 * nvec), :] = two_terms(
                    source[index[0, t]], source[index[0, t + 1]], matrix[t], matrix[t + 1])
        loop(0, slots // GROUP, step)

    products(segf, cols_s, flip)

    half = nchip * sub
    def keep(ref):
        def store(v, x):
            ref[pl.ds(v, half, stride=nvec), :] = x
        return store

    def pair_sum(q):
        part = pl.ds(pl.multiple_of(q * piece * size, piece * size), piece * size)
        return remote(other.at[part], partner.at[part], pair_send.at[1 + q], pair_recv.at[1 + q],
                      r, chip * 2 + 1 - core)
    npiece = chip // piece + 1
    collect(picks(place, (1 - core) * half, half), terms, slots, nvec, width, keep(other))
    loop(0, npiece, lambda q: pair_sum(q).start())
    collect(picks(place, core * half, half), terms, slots, nvec, width, keep(mine))
    pl.when(chip < split)(relay)
    loop(close, nchip, to_later)

    def rs_out(k):
        return remote(fixed.at[k, words], rsum.at[chip, words], rs_send.at[k], rs_recv.at[chip],
                      r, k * 2 + core)
    def rs_in(k):
        return remote(rsum.at[k, words], rsum.at[k, words], rs_send.at[k], rs_recv.at[k],
                      r, k * 2 + core)

    low = size // 2
    words = pl.ds(0, low + 1)
    def to_fixed(x):
        most = jnp.max(jnp.abs(x), axis=0, keepdims=True)
        power = jnp.ceil(jnp.log2(jnp.maximum(most, 2.0 ** -100)))
        code = jnp.round(x * (jnp.exp2(-power) * LIMIT)).astype(jnp.int32)
        word = jnp.left_shift(code[:low], 16) | (code[low:] & 0xFFFF)
        return jnp.concatenate([word, power.astype(jnp.int32)], 0)
    def from_fixed(ref):
        word = ref[0:low, :]
        code = jnp.concatenate([
            jnp.right_shift(word, 16), jnp.right_shift(jnp.left_shift(word, 16), 16)], 0)
        power = ref[low:low + 1, :].astype(F32)
        return code.astype(F32) * (jnp.exp2(power) * (1.0 / LIMIT))

    def send_rows(q):
        pair_sum(q).wait_recv()
        for u in range(piece):
            k = q * piece + u
            part = pl.ds(pl.multiple_of(k * size, size), size)
            x = mine[part, :] + partner[part, :]
            mine[part, :] = x
            fixed[k, 0:low + 1, :] = to_fixed(x)
        loop(q * piece, jnp.minimum((q + 1) * piece, chip), lambda k: rs_out(k).start())
    loop(0, npiece, send_rows)

    pl.when(chip >= split)(relay)

    pair_slab.wait_recv()
    for k in range(nchip):
        for m in range(2):
            block = slab[m, k].astype(F32)
            for s in range(sub):
                slabf[(k * 2 + m) * sub + s] = block[s * nvec:(s + 1) * nvec]

    products(slabf, rows_s, tv)
    def keep_cols(v, x):
        csum[pl.ds(v, nb, stride=nvec), :] = x
    collect(picks(b, 0, nb), terms, slots, nvec, width, keep_cols)
    for k in range(nrow):
        cfixed[k, 0:low + 1, :] = to_fixed(csum[k * size:(k + 1) * size, :])
    def cs_copy(d):
        k = row_at(d)
        return remote(cfixed.at[k, words], crecv.at[d, words], cs_send.at[d], cs_recv.at[d], k, c)
    loop(1, nrow, lambda d: cs_copy(d).start())

    total = jnp.concatenate(
        [own[s * nvec:(s + 1) * nvec] * ebuf[:, s * width:(s + 1) * width] for s in range(sub)], 0)
    total = total + mine[pl.ds(pl.multiple_of(chip * size, size), size), :]
    total = total + csum[pl.ds(pl.multiple_of(r * size, size), size), :]
    def add_cols(d, x):
        cs_copy(d).wait_recv()
        return x + from_fixed(crecv.at[d])
    def add_rows(k, x):
        rs_in(k).wait_recv()
        return x + from_fixed(rsum.at[k])
    total = lax.fori_loop(1, nrow, add_cols, total)
    total = lax.fori_loop(chip + 1, nchip, add_rows, total)
    for s in range(sub):
        out[:, s * width:(s + 1) * width] = total[s * nvec:(s + 1) * nvec].astype(BF)

    loop(1, nrow, lambda d: seg_copy(d).wait_send())
    loop(chip + 1, nchip, lambda k: slab_out(k).wait_send())
    pair_slab.wait_send()
    loop(0, npiece, lambda q: pair_sum(q).wait_send())
    loop(0, chip, lambda k: rs_out(k).wait_send())
    loop(1, nrow, lambda d: cs_copy(d).wait_send())


def body(vectors, energies, tiles, tile_rows, tile_cols, counts):
    nrow, ncol = lax.axis_size("row"), lax.axis_size("col")
    slots, width = tiles.shape[2], tiles.shape[3]
    nvec, own = vectors.shape
    sub = own // width
    nchip = ncol // 2
    any_, dma = pl.BlockSpec(memory_space=pl.ANY), pltpu.SemaphoreType.DMA
    return pl.pallas_call(
        functools.partial(kernel, nrow, ncol),
        out_shape=pltpu.VMEM(vectors.shape, BF),
        in_specs=[any_] * 6,
        out_specs=pl.BlockSpec(memory_space=pltpu.VMEM),
        scratch_shapes=[
            pltpu.VMEM((slots, width, width), BF),
            pltpu.VMEM((slots, width, width), BF),
            pltpu.VMEM((nvec, own), BF),
            pltpu.VMEM((1, own), F32),
            pltpu.SMEM((1, slots), jnp.int32),
            pltpu.VMEM((1, slots), jnp.int32),
            pltpu.SMEM((1, slots), jnp.int32),
            pltpu.VMEM((1, slots), jnp.int32),
            pltpu.SMEM((1, 1), jnp.int32),
            pltpu.VMEM((nrow, sub * nvec, width), BF),
            pltpu.VMEM((nrow * sub, nvec, width), F32),
            pltpu.VMEM((2, nchip, sub * nvec, width), BF),
            pltpu.VMEM((ncol * sub, nvec, width), F32),
            pltpu.VMEM((slots * nvec, width), F32),
            pltpu.VMEM((nchip * sub * nvec, width), F32),
            pltpu.VMEM((nchip * sub * nvec, width), F32),
            pltpu.VMEM((nchip * sub * nvec, width), F32),
            pltpu.VMEM((nchip, sub * nvec // 2 + 8, width), jnp.int32),
            pltpu.VMEM((nchip, sub * nvec // 2 + 8, width), jnp.int32),
            pltpu.VMEM((nrow * sub * nvec, width), F32),
            pltpu.VMEM((nrow, sub * nvec // 2 + 8, width), jnp.int32),
            pltpu.VMEM((nrow, sub * nvec // 2 + 8, width), jnp.int32),
            dma((slots // TURN,)), dma((7,)),
            dma((nrow,)), dma((nrow,)), dma((nchip,)), dma((nchip,)),
            dma((1 + PIECES,)), dma((1 + PIECES,)), dma((nchip,)), dma((nchip,)), dma((nrow,)), dma((nrow,)),
            pltpu.SemaphoreType.REGULAR((nchip,)),
        ],
        compiler_params=pltpu.CompilerParams(
            collective_id=0, has_side_effects=True, vmem_limit_bytes=56 * 2**20
        ),
    )(vectors, energies.reshape(1, own), tiles, tile_rows, tile_cols, counts)


def solution(mesh):
    placed = (
        P(None, ("col", "row")),
        P(("col", "row")),
        P("row", "col", None, None, None),
        P("row", "col", None),
        P("row", "col", None),
        P("row", "col"),
    )
    return jax.shard_map(
        body, mesh=mesh, in_specs=placed, out_specs=P(None, ("col", "row")), check_vma=False
    )
```

```python
import functools

import jax
import jax.numpy as jnp
from jax import lax
from jax.experimental import pallas as pl
from jax.experimental.pallas import tpu as pltpu
from jax.sharding import PartitionSpec as P

MESH = pl.DeviceIdType.MESH
BF, F32 = jnp.bfloat16, jnp.float32
GROUP = 256
TURN = 32
LIMIT = 32766.0
PIECES = 4


def remote(src, dst, send, recv, row, col):
    return pltpu.make_async_remote_copy(
        src_ref=src, dst_ref=dst, send_sem=send, recv_sem=recv,
        device_id=(row, col), device_id_type=MESH,
    )


def loop(lo, hi, step):
    lax.fori_loop(lo, hi, lambda i, c: (step(i), c)[1], 0)


def two_terms(x0, x1, t0, t1):
    zero = jnp.zeros_like(x0)
    left = jnp.concatenate([x0, zero], 0).astype(BF)
    right = jnp.concatenate([zero, x1], 0).astype(BF)
    both = jnp.concatenate([left, right], 1)
    return jnp.dot(both, jnp.concatenate([t0, t1], 0), preferred_element_type=F32)


def collect(picks, terms, slots, nvec, width, store):
    for v in range(nvec):
        term = terms[pl.ds(v, slots, stride=nvec), :]
        high = term.astype(BF)
        low = (term - high.astype(F32)).astype(BF)
        out = jnp.dot(picks[...], jnp.concatenate([high, low], 1), preferred_element_type=F32)
        store(v, out[:, :width] + out[:, width:])


def kernel(
    nrow, ncol,
    vec, en, tiles, rows, cols, cnt, out,
    tv, flip, vbuf, ebuf, rows_s, rows_v, cols_s, cols_v, cnt_s,
    pick_other, pick_mine, pick_cols, seg, segf, slab, slabf, terms, mine, other, partner, fixed, rsum, csum, cfixed, crecv,
    tile_sem, in_sem, seg_send, seg_recv, slab_send, slab_recv,
    pair_send, pair_recv, rs_send, rs_recv, cs_send, cs_recv, ready,
):
    slots, width = tv.shape[0], tv.shape[2]
    nvec = vec.shape[0]
    sub = vec.shape[1] // width
    nchip = ncol // 2
    r, c = lax.axis_index("row"), lax.axis_index("col")
    chip, core = c // 2, c % 2

    def row_at(d):
        return lax.rem(r + d, nrow)

    barrier = pltpu.get_barrier_semaphore()
    def greet(row, col):
        pl.semaphore_signal(barrier, inc=1, device_id=(row, col), device_id_type=MESH)
    loop(1, nrow, lambda d: greet(row_at(d), c))
    greet(r, chip * 2 + 1 - core)
    loop(chip + 1, nchip, lambda k: greet(r, k * 2 + core))

    nch = slots // TURN
    def tile_copy(g):
        part = pl.ds(pl.multiple_of(g * TURN, TURN), TURN)
        return pltpu.make_async_copy(tiles.at[0, 0, part], tv.at[part], tile_sem.at[g])
    small = [
        pltpu.make_async_copy(s, d, in_sem.at[k])
        for k, (s, d) in enumerate((
            (vec, vbuf), (cols.at[0], cols_s), (rows.at[0], rows_s),
            (cols.at[0], cols_v), (rows.at[0], rows_v), (cnt, cnt_s), (en, ebuf),
        ))
    ]
    for copy in small:
        copy.start()
    loop(0, nch, lambda g: tile_copy(g).start())

    small[0].wait()
    own = jnp.concatenate(
        [vbuf[:, s * width:(s + 1) * width].astype(F32) for s in range(sub)], 0
    )
    seg[r] = own.astype(BF)
    slab[core, chip] = own.astype(BF)

    def turn(g):
        tile_copy(g).wait()
        for u in range(TURN):
            flip[g * TURN + u] = tv[g * TURN + u].T
    def turn_all():
        loop(0, nch, turn)
    split = nchip // 2
    pl.semaphore_wait(barrier, nrow + chip)

    def seg_copy(d):
        return remote(seg.at[r], seg.at[r], seg_send.at[d], seg_recv.at[d], row_at(d), c)
    def slab_out(k):
        return remote(slab.at[core, chip], slab.at[core, chip], slab_send.at[k], slab_recv.at[chip],
                      r, k * 2 + core)
    def slab_in(k):
        return remote(slab.at[core, k], slab.at[core, k], slab_send.at[k], slab_recv.at[k],
                      r, k * 2 + core)
    def seg_start(k):
        @pl.when(k != r)
        def _():
            seg_copy(lax.rem(k + nrow - r, nrow)).start()
    loop(0, nrow, seg_start)
    loop(0, chip, lambda k: pl.semaphore_signal(
        ready.at[chip], inc=1, device_id=(r, k * 2 + core), device_id_type=MESH))

    for copy in small[1:]:
        copy.wait()
    live = lax.broadcasted_iota(jnp.int32, (1, slots), 1) < cnt_s[0, 0]
    a, b = rows_v[...], cols_v[...]
    place = (a // sub % 2) * (nchip * sub) + (a // (2 * sub)) * sub + a % sub
    place = jnp.where(live, place, -1)
    b = jnp.where(live, b, -1)

    def picks(targets, first, count):
        index = lax.broadcasted_iota(jnp.int32, (count, slots), 0) + first
        return (index == targets).astype(BF)
    half = nchip * sub
    nb = nrow * sub
    pick_other[...] = picks(place, (1 - core) * half, half)
    pick_mine[...] = picks(place, core * half, half)
    pick_cols[...] = picks(b, 0, nb)

    turn_all()

    pair_slab = remote(slab.at[core], slab.at[core], pair_send.at[0], pair_recv.at[0],
                       r, chip * 2 + 1 - core)
    size = sub * nvec
    piece = nchip // PIECES

    def relay():
        loop(0, chip, lambda k: slab_in(k).wait_recv())
        pair_slab.start()

    def to_later(k):
        pl.semaphore_wait(ready.at[k], 1)
        slab_out(k).start()

    first = chip < max(nchip // 8, 1)
    close = jnp.where(first, split, nchip)
    loop(chip + 1, close, to_later)

    loop(1, nrow, lambda d: seg_copy(d).wait_recv())
    for k in range(nrow):
        block = seg[k].astype(F32)
        for s in range(sub):
            segf[k * sub + s] = block[s * nvec:(s + 1) * nvec]

    def products(source, index, matrix):
        def step(g):
            for u in range(0, GROUP, 2):
                t = g * GROUP + u
                terms[pl.ds(pl.multiple_of(t * nvec, 2 * nvec), 2 * nvec), :] = two_terms(
                    source[index[0, t]], source[index[0, t + 1]], matrix[t], matrix[t + 1])
        loop(0, slots // GROUP, step)

    products(segf, cols_s, flip)

    def keep(ref):
        def store(v, x):
            ref[pl.ds(v, half, stride=nvec), :] = x
        return store

    def pair_sum(q):
        part = pl.ds(pl.multiple_of(q * piece * size, piece * size), piece * size)
        return remote(other.at[part], partner.at[part], pair_send.at[1 + q], pair_recv.at[1 + q],
                      r, chip * 2 + 1 - core)
    npiece = chip // piece + 1
    collect(pick_other, terms, slots, nvec, width, keep(other))
    loop(0, npiece, lambda q: pair_sum(q).start())
    collect(pick_mine, terms, slots, nvec, width, keep(mine))
    pl.when(chip < split)(relay)
    loop(close, nchip, to_later)

    def rs_out(k):
        return remote(fixed.at[k, words], rsum.at[chip, words], rs_send.at[k], rs_recv.at[chip],
                      r, k * 2 + core)
    def rs_in(k):
        return remote(rsum.at[k, words], rsum.at[k, words], rs_send.at[k], rs_recv.at[k],
                      r, k * 2 + core)

    low = size // 2
    words = pl.ds(0, low + 1)
    def to_fixed(x):
        most = jnp.max(jnp.abs(x), axis=0, keepdims=True)
        power = jnp.ceil(jnp.log2(jnp.maximum(most, 2.0 ** -100)))
        code = jnp.round(x * (jnp.exp2(-power) * LIMIT)).astype(jnp.int32)
        word = jnp.left_shift(code[:low], 16) | (code[low:] & 0xFFFF)
        return jnp.concatenate([word, power.astype(jnp.int32)], 0)
    def from_fixed(ref):
        word = ref[0:low, :]
        code = jnp.concatenate([
            jnp.right_shift(word, 16), jnp.right_shift(jnp.left_shift(word, 16), 16)], 0)
        power = ref[low:low + 1, :].astype(F32)
        return code.astype(F32) * (jnp.exp2(power) * (1.0 / LIMIT))

    def send_rows(q):
        pair_sum(q).wait_recv()
        for u in range(piece):
            k = q * piece + u
            part = pl.ds(pl.multiple_of(k * size, size), size)
            x = mine[part, :] + partner[part, :]
            mine[part, :] = x
            fixed[k, 0:low + 1, :] = to_fixed(x)
        loop(q * piece, jnp.minimum((q + 1) * piece, chip), lambda k: rs_out(k).start())
    loop(0, npiece, send_rows)

    pl.when(chip >= split)(relay)

    pair_slab.wait_recv()
    for k in range(nchip):
        for m in range(2):
            block = slab[m, k].astype(F32)
            for s in range(sub):
                slabf[(k * 2 + m) * sub + s] = block[s * nvec:(s + 1) * nvec]

    products(slabf, rows_s, tv)
    def keep_cols(v, x):
        csum[pl.ds(v, nb, stride=nvec), :] = x
    collect(pick_cols, terms, slots, nvec, width, keep_cols)
    for k in range(nrow):
        cfixed[k, 0:low + 1, :] = to_fixed(csum[k * size:(k + 1) * size, :])
    def cs_copy(d):
        k = row_at(d)
        return remote(cfixed.at[k, words], crecv.at[d, words], cs_send.at[d], cs_recv.at[d], k, c)
    def cs_start(k):
        @pl.when(k != r)
        def _():
            cs_copy(lax.rem(k + nrow - r, nrow)).start()
    loop(0, nrow, cs_start)

    loop(1, nrow, lambda d: seg_copy(d).wait_send())
    loop(chip + 1, nchip, lambda k: slab_out(k).wait_send())
    pair_slab.wait_send()
    loop(0, npiece, lambda q: pair_sum(q).wait_send())
    loop(0, chip, lambda k: rs_out(k).wait_send())
    loop(1, nrow, lambda d: cs_copy(d).wait_send())

    total = jnp.concatenate(
        [own[s * nvec:(s + 1) * nvec] * ebuf[:, s * width:(s + 1) * width] for s in range(sub)], 0)
    total = total + mine[pl.ds(pl.multiple_of(chip * size, size), size), :]
    total = total + csum[pl.ds(pl.multiple_of(r * size, size), size), :]
    def add_cols(d, x):
        cs_copy(d).wait_recv()
        return x + from_fixed(crecv.at[d])
    def add_rows(k, x):
        rs_in(k).wait_recv()
        return x + from_fixed(rsum.at[k])
    total = lax.fori_loop(1, nrow, add_cols, total)
    total = lax.fori_loop(chip + 1, split, add_rows, total)
    total = lax.fori_loop(0, jnp.minimum(split, nchip - 1 - chip),
                          lambda i, x: add_rows(nchip - 1 - i, x), total)
    for s in range(sub):
        out[:, s * width:(s + 1) * width] = total[s * nvec:(s + 1) * nvec].astype(BF)


def body(vectors, energies, tiles, tile_rows, tile_cols, counts):
    nrow, ncol = lax.axis_size("row"), lax.axis_size("col")
    slots, width = tiles.shape[2], tiles.shape[3]
    nvec, own = vectors.shape
    sub = own // width
    nchip = ncol // 2
    any_, dma = pl.BlockSpec(memory_space=pl.ANY), pltpu.SemaphoreType.DMA
    return pl.pallas_call(
        functools.partial(kernel, nrow, ncol),
        out_shape=pltpu.VMEM(vectors.shape, BF),
        in_specs=[any_] * 6,
        out_specs=pl.BlockSpec(memory_space=pltpu.VMEM),
        scratch_shapes=[
            pltpu.VMEM((slots, width, width), BF),
            pltpu.VMEM((slots, width, width), BF),
            pltpu.VMEM((nvec, own), BF),
            pltpu.VMEM((1, own), F32),
            pltpu.SMEM((1, slots), jnp.int32),
            pltpu.VMEM((1, slots), jnp.int32),
            pltpu.SMEM((1, slots), jnp.int32),
            pltpu.VMEM((1, slots), jnp.int32),
            pltpu.SMEM((1, 1), jnp.int32),
            pltpu.VMEM((nchip * sub, slots), BF),
            pltpu.VMEM((nchip * sub, slots), BF),
            pltpu.VMEM((nrow * sub, slots), BF),
            pltpu.VMEM((nrow, sub * nvec, width), BF),
            pltpu.VMEM((nrow * sub, nvec, width), F32),
            pltpu.VMEM((2, nchip, sub * nvec, width), BF),
            pltpu.VMEM((ncol * sub, nvec, width), F32),
            pltpu.VMEM((slots * nvec, width), F32),
            pltpu.VMEM((nchip * sub * nvec, width), F32),
            pltpu.VMEM((nchip * sub * nvec, width), F32),
            pltpu.VMEM((nchip * sub * nvec, width), F32),
            pltpu.VMEM((nchip, sub * nvec // 2 + 8, width), jnp.int32),
            pltpu.VMEM((nchip, sub * nvec // 2 + 8, width), jnp.int32),
            pltpu.VMEM((nrow * sub * nvec, width), F32),
            pltpu.VMEM((nrow, sub * nvec // 2 + 8, width), jnp.int32),
            pltpu.VMEM((nrow, sub * nvec // 2 + 8, width), jnp.int32),
            dma((slots // TURN,)), dma((7,)),
            dma((nrow,)), dma((nrow,)), dma((nchip,)), dma((nchip,)),
            dma((1 + PIECES,)), dma((1 + PIECES,)), dma((nchip,)), dma((nchip,)), dma((nrow,)), dma((nrow,)),
            pltpu.SemaphoreType.REGULAR((nchip,)),
        ],
        compiler_params=pltpu.CompilerParams(
            collective_id=0, has_side_effects=True, vmem_limit_bytes=56 * 2**20
        ),
    )(vectors, energies.reshape(1, own), tiles, tile_rows, tile_cols, counts)


def solution(mesh):
    placed = (
        P(None, ("col", "row")),
        P(("col", "row")),
        P("row", "col", None, None, None),
        P("row", "col", None),
        P("row", "col", None),
        P("row", "col"),
    )
    return jax.shard_map(
        body, mesh=mesh, in_specs=placed, out_specs=P(None, ("col", "row")), check_vma=False
    )
```

```python
import functools

import jax
import jax.numpy as jnp
from jax import lax
from jax.experimental import pallas as pl
from jax.experimental.pallas import tpu as pltpu
from jax.sharding import PartitionSpec as P

MESH = pl.DeviceIdType.MESH
BF, F32 = jnp.bfloat16, jnp.float32
GROUP = 256
TURN = 32
LIMIT = 32512.0
PIECES = 4


def remote(src, dst, send, recv, row, col):
    return pltpu.make_async_remote_copy(
        src_ref=src, dst_ref=dst, send_sem=send, recv_sem=recv,
        device_id=(row, col), device_id_type=MESH,
    )


def loop(lo, hi, step):
    lax.fori_loop(lo, hi, lambda i, c: (step(i), c)[1], 0)


def two_terms(x0, x1, t0, t1):
    zero = jnp.zeros_like(x0)
    left = jnp.concatenate([x0, zero], 0).astype(BF)
    right = jnp.concatenate([zero, x1], 0).astype(BF)
    both = jnp.concatenate([left, right], 1)
    return jnp.dot(both, jnp.concatenate([t0, t1], 0), preferred_element_type=F32)


def collect(picks, terms, slots, nvec, width, store):
    for v in range(nvec):
        term = terms[pl.ds(v, slots, stride=nvec), :]
        high = term.astype(BF)
        low = (term - high.astype(F32)).astype(BF)
        out = jnp.dot(picks[...], jnp.concatenate([high, low], 1), preferred_element_type=F32)
        store(v, out[:, :width] + out[:, width:])


def kernel(
    nrow, ncol,
    vec, en, tiles, rows, cols, cnt, out,
    tv, flip, vbuf, ebuf, rows_s, rows_v, cols_s, cols_v, cnt_s,
    pick_other, pick_mine, pick_cols, seg, segf, slab, slabf, terms, mine, other, partner, fixed, rsum, csum, cfixed, crecv,
    tile_sem, in_sem, seg_send, seg_recv, slab_send, slab_recv,
    pair_send, pair_recv, rs_send, rs_recv, cs_send, cs_recv, ready,
):
    slots, width = tv.shape[0], tv.shape[2]
    nvec = vec.shape[0]
    sub = vec.shape[1] // width
    nchip = ncol // 2
    r, c = lax.axis_index("row"), lax.axis_index("col")
    chip, core = c // 2, c % 2

    def row_at(d):
        return lax.rem(r + d, nrow)

    barrier = pltpu.get_barrier_semaphore()
    def greet(row, col):
        pl.semaphore_signal(barrier, inc=1, device_id=(row, col), device_id_type=MESH)
    loop(1, nrow, lambda d: greet(row_at(d), c))
    greet(r, chip * 2 + 1 - core)
    loop(chip + 1, nchip, lambda k: greet(r, k * 2 + core))

    nch = slots // TURN
    def tile_copy(g):
        part = pl.ds(pl.multiple_of(g * TURN, TURN), TURN)
        return pltpu.make_async_copy(tiles.at[0, 0, part], tv.at[part], tile_sem.at[g])
    small = [
        pltpu.make_async_copy(s, d, in_sem.at[k])
        for k, (s, d) in enumerate((
            (vec, vbuf), (cols.at[0], cols_s), (rows.at[0], rows_s),
            (cols.at[0], cols_v), (rows.at[0], rows_v), (cnt, cnt_s), (en, ebuf),
        ))
    ]
    for copy in small:
        copy.start()
    loop(0, nch, lambda g: tile_copy(g).start())

    small[0].wait()
    own = jnp.concatenate(
        [vbuf[:, s * width:(s + 1) * width].astype(F32) for s in range(sub)], 0
    )
    seg[r] = own.astype(BF)
    slab[core, chip] = own.astype(BF)

    def turn(g):
        tile_copy(g).wait()
        for u in range(TURN):
            flip[g * TURN + u] = tv[g * TURN + u].T
    def turn_all():
        loop(0, nch, turn)
    split = nchip // 2
    pl.semaphore_wait(barrier, nrow + chip)

    def seg_copy(d):
        return remote(seg.at[r], seg.at[r], seg_send.at[d], seg_recv.at[d], row_at(d), c)
    def slab_out(k):
        return remote(slab.at[core, chip], slab.at[core, chip], slab_send.at[k], slab_recv.at[chip],
                      r, k * 2 + core)
    def slab_in(k):
        return remote(slab.at[core, k], slab.at[core, k], slab_send.at[k], slab_recv.at[k],
                      r, k * 2 + core)
    def seg_start(k):
        @pl.when(k != r)
        def _():
            seg_copy(lax.rem(k + nrow - r, nrow)).start()
    loop(0, nrow, seg_start)
    loop(0, chip, lambda k: pl.semaphore_signal(
        ready.at[chip], inc=1, device_id=(r, k * 2 + core), device_id_type=MESH))

    for copy in small[1:]:
        copy.wait()
    live = lax.broadcasted_iota(jnp.int32, (1, slots), 1) < cnt_s[0, 0]
    a, b = rows_v[...], cols_v[...]
    place = (a // sub % 2) * (nchip * sub) + (a // (2 * sub)) * sub + a % sub
    place = jnp.where(live, place, -1)
    b = jnp.where(live, b, -1)

    def picks(targets, first, count):
        index = lax.broadcasted_iota(jnp.int32, (count, slots), 0) + first
        return (index == targets).astype(BF)
    half = nchip * sub
    nb = nrow * sub
    pick_other[...] = picks(place, (1 - core) * half, half)
    pick_mine[...] = picks(place, core * half, half)
    pick_cols[...] = picks(b, 0, nb)

    turn_all()

    pair_slab = remote(slab.at[core], slab.at[core], pair_send.at[0], pair_recv.at[0],
                       r, chip * 2 + 1 - core)
    size = sub * nvec
    piece = nchip // PIECES

    def relay():
        loop(0, chip, lambda k: slab_in(k).wait_recv())
        pair_slab.start()

    def to_later(k):
        pl.semaphore_wait(ready.at[k], 1)
        slab_out(k).start()

    first = chip < max(nchip // 8, 1)
    close = jnp.where(first, split, nchip)
    loop(chip + 1, close, to_later)

    loop(1, nrow, lambda d: seg_copy(d).wait_recv())
    for k in range(nrow):
        block = seg[k].astype(F32)
        for s in range(sub):
            segf[k * sub + s] = block[s * nvec:(s + 1) * nvec]

    def products(source, index, matrix):
        def step(g):
            for u in range(0, GROUP, 2):
                t = g * GROUP + u
                terms[pl.ds(pl.multiple_of(t * nvec, 2 * nvec), 2 * nvec), :] = two_terms(
                    source[index[0, t]], source[index[0, t + 1]], matrix[t], matrix[t + 1])
        loop(0, slots // GROUP, step)

    products(segf, cols_s, flip)

    def keep(ref):
        def store(v, x):
            ref[pl.ds(v, half, stride=nvec), :] = x
        return store

    def pair_sum(q):
        part = pl.ds(pl.multiple_of(q * piece * size, piece * size), piece * size)
        return remote(other.at[part], partner.at[part], pair_send.at[1 + q], pair_recv.at[1 + q],
                      r, chip * 2 + 1 - core)
    npiece = chip // piece + 1
    collect(pick_other, terms, slots, nvec, width, keep(other))
    loop(0, npiece, lambda q: pair_sum(q).start())
    collect(pick_mine, terms, slots, nvec, width, keep(mine))
    pl.when(chip < split)(relay)
    loop(close, nchip, to_later)

    def rs_out(k):
        return remote(fixed.at[k, words], rsum.at[chip, words], rs_send.at[k], rs_recv.at[chip],
                      r, k * 2 + core)
    def rs_in(k):
        return remote(rsum.at[k, words], rsum.at[k, words], rs_send.at[k], rs_recv.at[k],
                      r, k * 2 + core)

    low = size // 2
    words = pl.ds(0, low + 1)
    def to_fixed(x):
        most = jnp.max(jnp.abs(x), axis=0, keepdims=True)
        power = jnp.ceil(jnp.log2(jnp.maximum(most, 2.0 ** -100)))
        code = jnp.round(x * (jnp.exp2(-power) * LIMIT)).astype(jnp.int32)
        word = jnp.left_shift(code[:low], 16) | (code[low:] & 0xFFFF)
        return jnp.concatenate([word, power.astype(jnp.int32)], 0)
    def from_fixed(ref):
        word = ref[0:low, :]
        code = jnp.concatenate([
            jnp.right_shift(word, 16), jnp.right_shift(jnp.left_shift(word, 16), 16)], 0)
        power = ref[low:low + 1, :].astype(F32)
        return code.astype(F32) * (jnp.exp2(power) * (1.0 / LIMIT))

    def send_rows(q):
        pair_sum(q).wait_recv()
        for u in range(piece):
            k = q * piece + u
            part = pl.ds(pl.multiple_of(k * size, size), size)
            x = mine[part, :] + partner[part, :]
            mine[part, :] = x
            fixed[k, 0:low + 1, :] = to_fixed(x)
        loop(q * piece, jnp.minimum((q + 1) * piece, chip), lambda k: rs_out(k).start())
    loop(0, npiece, send_rows)

    pl.when(chip >= split)(relay)

    pair_slab.wait_recv()
    for k in range(nchip):
        for m in range(2):
            block = slab[m, k].astype(F32)
            for s in range(sub):
                slabf[(k * 2 + m) * sub + s] = block[s * nvec:(s + 1) * nvec]

    products(slabf, rows_s, tv)
    def keep_cols(v, x):
        csum[pl.ds(v, nb, stride=nvec), :] = x
    collect(pick_cols, terms, slots, nvec, width, keep_cols)
    for k in range(nrow):
        cfixed[k, 0:low + 1, :] = to_fixed(csum[k * size:(k + 1) * size, :])
    def cs_copy(d):
        k = row_at(d)
        return remote(cfixed.at[k, words], crecv.at[d, words], cs_send.at[d], cs_recv.at[d], k, c)
    def cs_start(k):
        @pl.when(k != r)
        def _():
            cs_copy(lax.rem(k + nrow - r, nrow)).start()
    loop(0, nrow, cs_start)

    loop(1, nrow, lambda d: seg_copy(d).wait_send())
    loop(chip + 1, nchip, lambda k: slab_out(k).wait_send())
    pair_slab.wait_send()
    loop(0, npiece, lambda q: pair_sum(q).wait_send())
    loop(0, chip, lambda k: rs_out(k).wait_send())
    loop(1, nrow, lambda d: cs_copy(d).wait_send())

    total = jnp.concatenate(
        [own[s * nvec:(s + 1) * nvec] * ebuf[:, s * width:(s + 1) * width] for s in range(sub)], 0)
    total = total + mine[pl.ds(pl.multiple_of(chip * size, size), size), :]
    total = total + csum[pl.ds(pl.multiple_of(r * size, size), size), :]
    def add_cols(d, x):
        cs_copy(d).wait_recv()
        return x + from_fixed(crecv.at[d])
    def add_rows(k, x):
        rs_in(k).wait_recv()
        return x + from_fixed(rsum.at[k])
    total = lax.fori_loop(1, nrow, add_cols, total)
    total = lax.fori_loop(chip + 1, split, add_rows, total)
    total = lax.fori_loop(0, jnp.minimum(split, nchip - 1 - chip),
                          lambda i, x: add_rows(nchip - 1 - i, x), total)
    for s in range(sub):
        out[:, s * width:(s + 1) * width] = total[s * nvec:(s + 1) * nvec].astype(BF)


def body(vectors, energies, tiles, tile_rows, tile_cols, counts):
    nrow, ncol = lax.axis_size("row"), lax.axis_size("col")
    slots, width = tiles.shape[2], tiles.shape[3]
    nvec, own = vectors.shape
    sub = own // width
    nchip = ncol // 2
    any_, dma = pl.BlockSpec(memory_space=pl.ANY), pltpu.SemaphoreType.DMA
    return pl.pallas_call(
        functools.partial(kernel, nrow, ncol),
        out_shape=pltpu.VMEM(vectors.shape, BF),
        in_specs=[any_] * 6,
        out_specs=pl.BlockSpec(memory_space=pltpu.VMEM),
        scratch_shapes=[
            pltpu.VMEM((slots, width, width), BF),
            pltpu.VMEM((slots, width, width), BF),
            pltpu.VMEM((nvec, own), BF),
            pltpu.VMEM((1, own), F32),
            pltpu.SMEM((1, slots), jnp.int32),
            pltpu.VMEM((1, slots), jnp.int32),
            pltpu.SMEM((1, slots), jnp.int32),
            pltpu.VMEM((1, slots), jnp.int32),
            pltpu.SMEM((1, 1), jnp.int32),
            pltpu.VMEM((nchip * sub, slots), BF),
            pltpu.VMEM((nchip * sub, slots), BF),
            pltpu.VMEM((nrow * sub, slots), BF),
            pltpu.VMEM((nrow, sub * nvec, width), BF),
            pltpu.VMEM((nrow * sub, nvec, width), F32),
            pltpu.VMEM((2, nchip, sub * nvec, width), BF),
            pltpu.VMEM((ncol * sub, nvec, width), F32),
            pltpu.VMEM((slots * nvec, width), F32),
            pltpu.VMEM((nchip * sub * nvec, width), F32),
            pltpu.VMEM((nchip * sub * nvec, width), F32),
            pltpu.VMEM((nchip * sub * nvec, width), F32),
            pltpu.VMEM((nchip, sub * nvec // 2 + 8, width), jnp.int32),
            pltpu.VMEM((nchip, sub * nvec // 2 + 8, width), jnp.int32),
            pltpu.VMEM((nrow * sub * nvec, width), F32),
            pltpu.VMEM((nrow, sub * nvec // 2 + 8, width), jnp.int32),
            pltpu.VMEM((nrow, sub * nvec // 2 + 8, width), jnp.int32),
            dma((slots // TURN,)), dma((7,)),
            dma((nrow,)), dma((nrow,)), dma((nchip,)), dma((nchip,)),
            dma((1 + PIECES,)), dma((1 + PIECES,)), dma((nchip,)), dma((nchip,)), dma((nrow,)), dma((nrow,)),
            pltpu.SemaphoreType.REGULAR((nchip,)),
        ],
        compiler_params=pltpu.CompilerParams(
            collective_id=0, has_side_effects=True, vmem_limit_bytes=56 * 2**20
        ),
    )(vectors, energies.reshape(1, own), tiles, tile_rows, tile_cols, counts)


def solution(mesh):
    placed = (
        P(None, ("col", "row")),
        P(("col", "row")),
        P("row", "col", None, None, None),
        P("row", "col", None),
        P("row", "col", None),
        P("row", "col"),
    )
    return jax.shard_map(
        body, mesh=mesh, in_specs=placed, out_specs=P(None, ("col", "row")), check_vma=False
    )
```

```python
import functools

import jax
import jax.numpy as jnp
from jax import lax
from jax.experimental import pallas as pl
from jax.experimental.pallas import tpu as pltpu
from jax.sharding import PartitionSpec as P

MESH = pl.DeviceIdType.MESH
BF, F32 = jnp.bfloat16, jnp.float32
GROUP = 256
MUTUAL = 2
TURN = 32
LIMIT = 32512.0
PIECES = 4


def remote(src, dst, send, recv, row, col):
    return pltpu.make_async_remote_copy(
        src_ref=src, dst_ref=dst, send_sem=send, recv_sem=recv,
        device_id=(row, col), device_id_type=MESH,
    )


def loop(lo, hi, step):
    lax.fori_loop(lo, hi, lambda i, c: (step(i), c)[1], 0)


def two_terms(x0, x1, t0, t1):
    zero = jnp.zeros_like(x0)
    left = jnp.concatenate([x0, zero], 0).astype(BF)
    right = jnp.concatenate([zero, x1], 0).astype(BF)
    both = jnp.concatenate([left, right], 1)
    return jnp.dot(both, jnp.concatenate([t0, t1], 0), preferred_element_type=F32)


def collect(picks, terms, slots, nvec, width, store):
    for v in range(nvec):
        term = terms[pl.ds(v, slots, stride=nvec), :]
        high = term.astype(BF)
        low = (term - high.astype(F32)).astype(BF)
        out = jnp.dot(picks[...], jnp.concatenate([high, low], 1), preferred_element_type=F32)
        store(v, out[:, :width] + out[:, width:])


def kernel(
    nrow, ncol,
    vec, en, tiles, rows, cols, cnt, out,
    tv, flip, vbuf, ebuf, rows_s, rows_v, cols_s, cols_v, cnt_s,
    pick_other, pick_mine, pick_cols, seg, segf, slab, slabf, terms, mine, other, partner, fixed, rsum, csum, cfixed, crecv,
    tile_sem, in_sem, seg_send, seg_recv, slab_send, slab_recv,
    pair_send, pair_recv, rs_send, rs_recv, cs_send, cs_recv, ready,
):
    slots, width = tv.shape[0], tv.shape[2]
    nvec = vec.shape[0]
    sub = vec.shape[1] // width
    nchip = ncol // 2
    r, c = lax.axis_index("row"), lax.axis_index("col")
    chip, core = c // 2, c % 2

    def row_at(d):
        return lax.rem(r + d, nrow)

    barrier = pltpu.get_barrier_semaphore()
    def greet(row, col):
        pl.semaphore_signal(barrier, inc=1, device_id=(row, col), device_id_type=MESH)
    loop(1, nrow, lambda d: greet(row_at(d), c))
    greet(r, chip * 2 + 1 - core)
    loop(chip + 1, nchip, lambda k: greet(r, k * 2 + core))
    split = nchip // 2
    mutual = (r < MUTUAL) & (chip >= split)
    loop(jnp.where(mutual, split, chip), chip, lambda k: greet(r, k * 2 + core))

    nch = slots // TURN
    def tile_copy(g):
        part = pl.ds(pl.multiple_of(g * TURN, TURN), TURN)
        return pltpu.make_async_copy(tiles.at[0, 0, part], tv.at[part], tile_sem.at[g])
    small = [
        pltpu.make_async_copy(s, d, in_sem.at[k])
        for k, (s, d) in enumerate((
            (vec, vbuf), (cols.at[0], cols_s), (rows.at[0], rows_s),
            (cols.at[0], cols_v), (rows.at[0], rows_v), (cnt, cnt_s), (en, ebuf),
        ))
    ]
    for copy in small:
        copy.start()
    loop(0, nch, lambda g: tile_copy(g).start())

    small[0].wait()
    own = jnp.concatenate(
        [vbuf[:, s * width:(s + 1) * width].astype(F32) for s in range(sub)], 0
    )
    seg[r] = own.astype(BF)
    slab[core, chip] = own.astype(BF)

    def turn(g):
        tile_copy(g).wait()
        for u in range(TURN):
            flip[g * TURN + u] = tv[g * TURN + u].T
    def turn_all():
        loop(0, nch, turn)
    pl.semaphore_wait(barrier, nrow + jnp.where(mutual, nchip - 1, chip))

    def seg_copy(d):
        return remote(seg.at[r], seg.at[r], seg_send.at[d], seg_recv.at[d], row_at(d), c)
    def slab_out(k):
        return remote(slab.at[core, chip], slab.at[core, chip], slab_send.at[k], slab_recv.at[chip],
                      r, k * 2 + core)
    def slab_in(k):
        return remote(slab.at[core, k], slab.at[core, k], slab_send.at[k], slab_recv.at[k],
                      r, k * 2 + core)
    def seg_start(k):
        @pl.when(k != r)
        def _():
            seg_copy(lax.rem(k + nrow - r, nrow)).start()
    loop(0, nrow, seg_start)
    loop(jnp.where(mutual, chip + 1, nchip), nchip, lambda k: slab_out(k).start())
    loop(0, jnp.where(mutual, split, chip), lambda k: pl.semaphore_signal(
        ready.at[chip], inc=1, device_id=(r, k * 2 + core), device_id_type=MESH))

    for copy in small[1:]:
        copy.wait()
    live = lax.broadcasted_iota(jnp.int32, (1, slots), 1) < cnt_s[0, 0]
    a, b = rows_v[...], cols_v[...]
    place = (a // sub % 2) * (nchip * sub) + (a // (2 * sub)) * sub + a % sub
    place = jnp.where(live, place, -1)
    b = jnp.where(live, b, -1)

    def picks(targets, first, count):
        index = lax.broadcasted_iota(jnp.int32, (count, slots), 0) + first
        return (index == targets).astype(BF)
    half = nchip * sub
    nb = nrow * sub
    pick_other[...] = picks(place, (1 - core) * half, half)
    pick_mine[...] = picks(place, core * half, half)
    pick_cols[...] = picks(b, 0, nb)

    turn_all()

    pair_slab = remote(slab.at[core], slab.at[core], pair_send.at[0], pair_recv.at[0],
                       r, chip * 2 + 1 - core)
    size = sub * nvec
    piece = nchip // PIECES

    def relay():
        loop(0, chip, lambda k: slab_in(k).wait_recv())
        pair_slab.start()

    def to_later(k):
        pl.semaphore_wait(ready.at[k], 1)
        slab_out(k).start()

    first = chip < max(nchip // 8, 1)
    close = jnp.where(first, split, nchip)
    loop(jnp.where(mutual, nchip, chip + 1), close, to_later)

    def spread_seg(k):
        block = seg[k].astype(F32)
        for s in range(sub):
            segf[k * sub + s] = block[s * nvec:(s + 1) * nvec]
    spread_seg(r)
    def seg_arrives(d):
        seg_copy(d).wait_recv()
        spread_seg(lax.rem(r + nrow - d, nrow))
    loop(1, nrow, seg_arrives)

    def products(source, index, matrix):
        def step(g):
            for u in range(0, GROUP, 2):
                t = g * GROUP + u
                terms[pl.ds(pl.multiple_of(t * nvec, 2 * nvec), 2 * nvec), :] = two_terms(
                    source[index[0, t]], source[index[0, t + 1]], matrix[t], matrix[t + 1])
        loop(0, slots // GROUP, step)

    products(segf, cols_s, flip)

    def keep(ref):
        def store(v, x):
            ref[pl.ds(v, half, stride=nvec), :] = x
        return store

    def pair_sum(q):
        part = pl.ds(pl.multiple_of(q * piece * size, piece * size), piece * size)
        return remote(other.at[part], partner.at[part], pair_send.at[1 + q], pair_recv.at[1 + q],
                      r, chip * 2 + 1 - core)
    npiece = chip // piece + 1
    collect(pick_other, terms, slots, nvec, width, keep(other))
    loop(0, npiece, lambda q: pair_sum(q).start())
    collect(pick_mine, terms, slots, nvec, width, keep(mine))
    pl.when(chip < split)(relay)
    loop(close, nchip, to_later)

    def rs_out(k):
        return remote(fixed.at[k, words], rsum.at[chip, words], rs_send.at[k], rs_recv.at[chip],
                      r, k * 2 + core)
    def rs_in(k):
        return remote(rsum.at[k, words], rsum.at[k, words], rs_send.at[k], rs_recv.at[k],
                      r, k * 2 + core)

    low = size // 2
    words = pl.ds(0, low + 1)
    def to_fixed(x):
        most = jnp.max(jnp.abs(x), axis=0, keepdims=True)
        power = jnp.ceil(jnp.log2(jnp.maximum(most, 2.0 ** -100)))
        code = jnp.round(x * (jnp.exp2(-power) * LIMIT)).astype(jnp.int32)
        word = jnp.left_shift(code[:low], 16) | (code[low:] & 0xFFFF)
        return jnp.concatenate([word, power.astype(jnp.int32)], 0)
    def from_fixed(ref):
        word = ref[0:low, :]
        code = jnp.concatenate([
            jnp.right_shift(word, 16), jnp.right_shift(jnp.left_shift(word, 16), 16)], 0)
        power = ref[low:low + 1, :].astype(F32)
        return code.astype(F32) * (jnp.exp2(power) * (1.0 / LIMIT))

    def send_rows(q):
        pair_sum(q).wait_recv()
        for u in range(piece):
            k = q * piece + u
            part = pl.ds(pl.multiple_of(k * size, size), size)
            x = mine[part, :] + partner[part, :]
            mine[part, :] = x
            fixed[k, 0:low + 1, :] = to_fixed(x)
        loop(q * piece, jnp.minimum((q + 1) * piece, chip), lambda k: rs_out(k).start())
    loop(0, npiece, send_rows)

    pl.when(chip >= split)(relay)

    def spread_slab(m):
        for k in range(nchip):
            block = slab[m, k].astype(F32)
            for s in range(sub):
                slabf[(k * 2 + m) * sub + s] = block[s * nvec:(s + 1) * nvec]
    spread_slab(core)
    pair_slab.wait_recv()
    spread_slab(1 - core)

    products(slabf, rows_s, tv)
    def keep_cols(v, x):
        csum[pl.ds(v, nb, stride=nvec), :] = x
    collect(pick_cols, terms, slots, nvec, width, keep_cols)
    for k in range(nrow):
        cfixed[k, 0:low + 1, :] = to_fixed(csum[k * size:(k + 1) * size, :])
    def cs_copy(d):
        k = row_at(d)
        return remote(cfixed.at[k, words], crecv.at[d, words], cs_send.at[d], cs_recv.at[d], k, c)
    def cs_start(k):
        @pl.when(k != r)
        def _():
            cs_copy(lax.rem(k + nrow - r, nrow)).start()
    loop(0, nrow, cs_start)

    loop(1, nrow, lambda d: seg_copy(d).wait_send())
    loop(chip + 1, nchip, lambda k: slab_out(k).wait_send())
    pair_slab.wait_send()
    loop(0, npiece, lambda q: pair_sum(q).wait_send())
    loop(0, chip, lambda k: rs_out(k).wait_send())
    loop(1, nrow, lambda d: cs_copy(d).wait_send())

    total = jnp.concatenate(
        [own[s * nvec:(s + 1) * nvec] * ebuf[:, s * width:(s + 1) * width] for s in range(sub)], 0)
    total = total + mine[pl.ds(pl.multiple_of(chip * size, size), size), :]
    total = total + csum[pl.ds(pl.multiple_of(r * size, size), size), :]
    def add_cols(d, x):
        cs_copy(d).wait_recv()
        return x + from_fixed(crecv.at[d])
    def add_rows(k, x):
        rs_in(k).wait_recv()
        return x + from_fixed(rsum.at[k])
    total = lax.fori_loop(1, nrow, add_cols, total)
    total = lax.fori_loop(chip + 1, split, add_rows, total)
    total = lax.fori_loop(0, jnp.minimum(split, nchip - 1 - chip),
                          lambda i, x: add_rows(nchip - 1 - i, x), total)
    for s in range(sub):
        out[:, s * width:(s + 1) * width] = total[s * nvec:(s + 1) * nvec].astype(BF)


def body(vectors, energies, tiles, tile_rows, tile_cols, counts):
    nrow, ncol = lax.axis_size("row"), lax.axis_size("col")
    slots, width = tiles.shape[2], tiles.shape[3]
    nvec, own = vectors.shape
    sub = own // width
    nchip = ncol // 2
    any_, dma = pl.BlockSpec(memory_space=pl.ANY), pltpu.SemaphoreType.DMA
    return pl.pallas_call(
        functools.partial(kernel, nrow, ncol),
        out_shape=pltpu.VMEM(vectors.shape, BF),
        in_specs=[any_] * 6,
        out_specs=pl.BlockSpec(memory_space=pltpu.VMEM),
        scratch_shapes=[
            pltpu.VMEM((slots, width, width), BF),
            pltpu.VMEM((slots, width, width), BF),
            pltpu.VMEM((nvec, own), BF),
            pltpu.VMEM((1, own), F32),
            pltpu.SMEM((1, slots), jnp.int32),
            pltpu.VMEM((1, slots), jnp.int32),
            pltpu.SMEM((1, slots), jnp.int32),
            pltpu.VMEM((1, slots), jnp.int32),
            pltpu.SMEM((1, 1), jnp.int32),
            pltpu.VMEM((nchip * sub, slots), BF),
            pltpu.VMEM((nchip * sub, slots), BF),
            pltpu.VMEM((nrow * sub, slots), BF),
            pltpu.VMEM((nrow, sub * nvec, width), BF),
            pltpu.VMEM((nrow * sub, nvec, width), F32),
            pltpu.VMEM((2, nchip, sub * nvec, width), BF),
            pltpu.VMEM((ncol * sub, nvec, width), F32),
            pltpu.VMEM((slots * nvec, width), F32),
            pltpu.VMEM((nchip * sub * nvec, width), F32),
            pltpu.VMEM((nchip * sub * nvec, width), F32),
            pltpu.VMEM((nchip * sub * nvec, width), F32),
            pltpu.VMEM((nchip, sub * nvec // 2 + 8, width), jnp.int32),
            pltpu.VMEM((nchip, sub * nvec // 2 + 8, width), jnp.int32),
            pltpu.VMEM((nrow * sub * nvec, width), F32),
            pltpu.VMEM((nrow, sub * nvec // 2 + 8, width), jnp.int32),
            pltpu.VMEM((nrow, sub * nvec // 2 + 8, width), jnp.int32),
            dma((slots // TURN,)), dma((7,)),
            dma((nrow,)), dma((nrow,)), dma((nchip,)), dma((nchip,)),
            dma((1 + PIECES,)), dma((1 + PIECES,)), dma((nchip,)), dma((nchip,)), dma((nrow,)), dma((nrow,)),
            pltpu.SemaphoreType.REGULAR((nchip,)),
        ],
        compiler_params=pltpu.CompilerParams(
            collective_id=0, has_side_effects=True, vmem_limit_bytes=56 * 2**20
        ),
    )(vectors, energies.reshape(1, own), tiles, tile_rows, tile_cols, counts)


def solution(mesh):
    placed = (
        P(None, ("col", "row")),
        P(("col", "row")),
        P("row", "col", None, None, None),
        P("row", "col", None),
        P("row", "col", None),
        P("row", "col"),
    )
    return jax.shard_map(
        body, mesh=mesh, in_specs=placed, out_specs=P(None, ("col", "row")), check_vma=False
    )
```
